32 devices in a mesh: pb: 8 (over z, x), ka: 4 (over y, core).
Axes of the slice: x: 2, y: 2, z: 4, core: 2. Of those that a mesh axis runs over, the one named last changes fastest.
Arguments:
- valence: float32 [208, 64, 1024], P('pb', 'ka'), may hold values from -6 to 6
- conduction: bfloat16 [208, 196, 1024], P('pb', None, 'ka'), may hold values from -0.0024414062 to 0.0024414062
- screened: float32 [8, 1024, 1024], P('pb'), may hold values from -1 to 3, as said below
- momentum: int32 [208, 1], P('pb'), may hold values from 0 to 7; in each aligned block of 26 rows (0 to 25, 26 to 51, ...) at most 6 rows name the same one
- kpairs: int32 [208, 2], P('pb'), may hold values from 0 to 7
- kpoint_slot: int32 [8], replicated, may hold values from 0 to 7, each once
- trial_blocks: float32 [8, 14336], P('pb', 'ka'), may hold values from -6 to 6
Outputs:
- response: float32 [8, 14336], P('pb', 'ka')
The draws below stay inside these ranges and needn't reach their ends.
Inputs may be any that keep to these rules, and one draw needn't show every extreme that they name: Among the k-pairs of one index of pb (rows i * 26 to (i + 1) * 26 - 1), at most 6 share a momentum transfer. `kpoint_slot`: each row number appears once. `screened`: each matrix is symmetric.
All inputs are finite; a program needn't handle non-finite values.
Results may differ from the reference program's by a relative error of at most 0.0003.
Values sent between devices are 32-bit elements; how exact they have to be, the bound alone decides.
A program may use at most 128 MiB of HBM per device.

```python
import math
import jax
import jax.numpy as jnp
import numpy as np
from jax import lax

NG = 1024
VB = 8
CB = 14
NTRIAL = 128
PAIR_DEV = 26
VP = 64
CP = 196
VC = 112
Q = 8
PAIRS = 208
NK = 8
CAP = 6


def draw_screened(key, part):
    key_diag = jax.random.fold_in(key, 11)
    key_off = jax.random.fold_in(key, 12)
    diagonal = jnp.exp(jax.random.uniform(key_diag, (Q, NG), jnp.float32, math.log(0.5), math.log(2.0)))
    jitter = jnp.clip(jax.random.normal(key_off, (Q, NG, NG), jnp.float32), -4.0, 4.0)
    symmetric = (jitter + jnp.swapaxes(jitter, 1, 2)) * (0.25 / math.sqrt(NG))
    identity = jnp.eye(NG, dtype=jnp.float32)
    return symmetric + diagonal[:, :, None] * identity[None, :, :]


def touch_ends(array, rng, least, high):
    index_at = [jax.random.randint(jax.random.fold_in(rng, axis), (), 0, length) for axis, length in enumerate(array.shape)]
    longest = array.shape.index(max(array.shape))
    neighbour = index_at[:longest] + [(index_at[longest] + 1) % array.shape[longest]] + index_at[longest + 1:]
    return array.at[tuple(index_at)].set(least).at[tuple(neighbour)].set(high)


def shard_levels(rng, extent, split, least, largest):
    gain, own = 1.0, jax.random.fold_in(rng, 6)
    for position, shards_of in split:
        draws = jnp.exp(jax.random.uniform(jax.random.fold_in(own, position), (shards_of,), jnp.float32, least / len(split), largest / len(split)))
        gain = gain * jnp.repeat(draws, extent[position] // shards_of).reshape([-1 if axis == position else 1 for axis in range(len(extent))])
    return gain


def routed_block(own_key, own, number, rows, number_of, top, most, skew):
    ranking = jax.random.permutation(own_key, number_of)
    crowded, usual = load_shares(number_of, rows * top, most, skew, True), load_shares(number_of, rows * top, most, skew, False)
    places = jnp.arange(number_of)

    def named(sizes, turn):
        used = int((sizes > 0).sum())
        fixed = max(1, used // 4)
        passed = fixed + (places - fixed + turn * (used - fixed)) % max(1, number_of - fixed)
        return jnp.zeros((number_of,), jnp.int32).at[ranking[jnp.where(places < fixed, places, passed)]].set(jnp.asarray(sizes, jnp.int32))

    sizes = jnp.where(number % 4 == 0, named(crowded, number // 4), named(usual, number - number // 4 - 1))
    mixed = jax.random.permutation(jax.random.fold_in(own, 3), number_of)
    donor, taker = mixed[0:number_of // 2 * 2:2], mixed[1:number_of // 2 * 2:2]
    margin = jnp.minimum(sizes[donor] - 1, most - sizes[taker]) // 2
    margin = jnp.where((donor == ranking[0]) | (taker == ranking[0]) | (sizes[taker] == 0), 0, jnp.maximum(margin, 0))
    passed = jax.random.randint(jax.random.fold_in(own, 4), (number_of // 2,), 0, 1 << 20) % (margin + 1)
    sizes = sizes.at[donor].add(-passed).at[taker].add(passed)
    labels = jnp.searchsorted(jnp.cumsum(sizes), jnp.arange(rows * top), side="right").astype(jnp.int32)
    grid = labels.reshape(top, rows).T
    grid = grid[jax.random.permutation(jax.random.fold_in(own, 1), rows)]
    turn = jax.random.randint(jax.random.fold_in(own, 2), (rows, 1), 0, top)
    return jnp.take_along_axis(grid, (jnp.arange(top)[None, :] + turn) % top, axis=1)


def load_shares(number_of, total, most, lean, full):
    portions = [(1 << 20) // math.isqrt(standing ** lean) + 1 for standing in range(1, number_of + 1)]
    largest = most if full else min(most, max(-(-total // number_of), total * portions[0] // sum(portions)))
    least = 1 if total - largest >= number_of - 1 else 0
    holding, surplus = [largest] + [least] * (number_of - 1), total - largest - least * (number_of - 1)
    while surplus > 0:
        candidates = [i for i in range(1, number_of) if holding[i] < largest] or [i for i in range(1, number_of) if holding[i] < most]
        pool, left = sum([portions[i] for i in candidates]), surplus
        for i in candidates:
            more = min(most - holding[i], max(1, left * portions[i] // pool), surplus)
            holding[i] = holding[i] + more
            surplus = surplus - more
    return np.array(holding)


def bell_draw(key, dims, width, limit, cuts=(), kind=jnp.bfloat16):
    values = jax.random.normal(key, dims, jnp.float32) * width
    if len(cuts) > 0:
        values = shard_levels(key, dims, cuts, -0.22, 0.18) * values
    return jnp.clip(values, min=-limit, max=limit).astype(kind)


def setup_inputs(seed: int = 0) -> dict:
    streams_of = jax.random.split(jax.random.key(seed), 8)
    valence = bell_draw(streams_of[0], (PAIRS, VP, NG), 1.0, 6.0, ((0, 8), (1, 4)), jnp.float32)
    conduction = bell_draw(streams_of[1], (PAIRS, CP, NG), (NG * VC * 2 * PAIR_DEV) ** -0.5, 0.0024414062, ((0, 8), (2, 4)))
    screened = draw_screened(jax.random.fold_in(streams_of[7], 71), 0)
    momentum_keys = jax.random.split(jax.random.fold_in(streams_of[3], 1), PAIRS // PAIR_DEV)
    momentum_turns = jax.random.permutation(jax.random.fold_in(streams_of[3], 3), PAIRS // PAIR_DEV)
    momentum = jax.vmap(lambda own, number: routed_block(jax.random.fold_in(streams_of[3], 2), own, number, PAIR_DEV, Q, 1, CAP, 2))(momentum_keys, momentum_turns).reshape((PAIRS, 1))
    kpairs = touch_ends(jax.random.randint(streams_of[4], (PAIRS, 2), 0, NK), jax.random.fold_in(streams_of[4], 1), 0, NK - 1).astype(jnp.int32)
    kpoint_slot = jax.random.permutation(streams_of[5], NK).astype(jnp.int32)
    trial_blocks = bell_draw(streams_of[6], (NK, NTRIAL * VC), 1.0, 6.0, ((0, 8), (1, 4)), jnp.float32)
    return dict(valence=valence, conduction=conduction, screened=screened, momentum=momentum, kpairs=kpairs, kpoint_slot=kpoint_slot, trial_blocks=trial_blocks)


def reference(valence, conduction, screened, momentum, kpairs, kpoint_slot, trial_blocks):
    highest = lax.Precision.HIGHEST

    def screen_pair(items):
        rows_in, conduct, index = items
        matrix = lax.dynamic_index_in_dim(screened, index, 0, keepdims=False)
        screened_rows = jnp.dot(rows_in, matrix, precision=highest, preferred_element_type=jnp.float32)
        conduct_wide = conduct.astype(jnp.float32)
        return jnp.dot(screened_rows, conduct_wide.T, precision=highest, preferred_element_type=jnp.float32)

    kernel = lax.map(screen_pair, (valence, conduction, momentum[:, 0].astype(jnp.int32)))
    kernel_blocks = kernel.reshape(PAIRS, VB, VB, CB, CB)
    slot_near = jnp.take(kpoint_slot, kpairs[:, 0].astype(jnp.int32)).astype(jnp.int32)
    slot_far = jnp.take(kpoint_slot, kpairs[:, 1].astype(jnp.int32)).astype(jnp.int32)
    blocks = trial_blocks.reshape(NK, NTRIAL, VB, CB)
    near_trials = jnp.take(blocks, slot_near, axis=0)
    far_trials = jnp.take(blocks, slot_far, axis=0)
    direct = jnp.einsum("pvwcd,pnwd->pnvc", kernel_blocks, far_trials, precision=highest)
    mirror = jnp.einsum("pvwcd,pnvc->pnwd", kernel_blocks, near_trials, precision=highest)
    result = jnp.zeros((NK, NTRIAL, VB, CB), jnp.float32)
    result = result.at[slot_near].add(direct)
    result = result.at[slot_far].add(mirror)
    return result.reshape(NK, NTRIAL * VB * CB)
```

```python
import functools

import jax
import jax.numpy as jnp
from jax import lax
from jax.experimental import pallas as pl
from jax.experimental.pallas import tpu as pltpu
from jax.sharding import PartitionSpec as P

VB = 8
CB = 14
MESH = pl.DeviceIdType.MESH
NT = (((1,), (1,)), ((), ()))


def dot_nt(a, b):
    return lax.dot_general(a, b, NT, preferred_element_type=jnp.float32)


def halves(x):
    high = x.astype(jnp.bfloat16)
    return high, (x - high.astype(jnp.float32)).astype(jnp.bfloat16)


def ring_index(place, n):
    return jnp.where(place < n // 2, 2 * place, 2 * (n - 1 - place) + 1)


def kernel_blocks_kernel(
    n, parts, capacity,
    source_ref, v_ref, c_ref, w_ref, x_ref,
    k_ref, xout_ref,
    w_all, v_all, v_high, v_low, g_high, g_low, k_part, k_in, x_all,
    local_sems, v_send, v_recv, ring_send, ring_recv, k_send, k_recv, x_send, x_recv, xk_send, xk_recv,
):
    pb, ka = lax.axis_index("pb"), lax.axis_index("ka")
    place = jnp.where(pb % 2 == 0, pb // 2, n - 1 - pb // 2)
    right = ring_index((place + 1) % n, n)
    left = ring_index((place + n - 1) % n, n)
    partner = ka + 1 - 2 * (ka % 2)
    across = (ka + 2) % parts
    rows = v_ref.shape[1]
    depth = w_all.shape[1]
    pairs = v_ref.shape[0]

    own_w = pltpu.make_async_copy(w_ref.at[0, pl.ds(pl.multiple_of(ka * depth, depth), depth), :], w_all.at[place], local_sems.at[0])
    own_v = pltpu.make_async_copy(v_ref, v_all.at[ka], local_sems.at[1])
    own_w.start()
    own_v.start()
    x_all[ka, pb] = x_ref[...]

    barrier = pltpu.get_barrier_semaphore()
    for d in range(1, n):
        pl.semaphore_signal(barrier, inc=1, device_id=((pb + d) % n, ka), device_id_type=MESH)
    for d in range(1, parts):
        pl.semaphore_signal(barrier, inc=1, device_id=(pb, (ka + d) % parts), device_id_type=MESH)
    pl.semaphore_wait(barrier, n + parts - 2)

    def remote(src, dst, send, recv, to):
        return pltpu.make_async_remote_copy(src_ref=src, dst_ref=dst, send_sem=send, recv_sem=recv, device_id=to, device_id_type=MESH)

    def ring(step):
        ahead = (place + n - step) % n
        behind = (place + step) % n
        if step < n // 2 - 1:
            go, back = w_all.at[ahead], w_all.at[behind]
        else:
            go = w_all.at[ahead, pl.ds(0, depth // 2)]
            back = w_all.at[behind, pl.ds(depth // 2, depth // 2)]
        return (
            remote(go, go, ring_send.at[step, 0], ring_recv.at[step, 0], (right, ka)),
            remote(back, back, ring_send.at[step, 1], ring_recv.at[step, 1], (left, ka)),
        )

    own_v.wait()
    v_across = remote(v_all.at[ka], v_all.at[ka], v_send.at[1], v_recv.at[1], (pb, across))
    v_partner = remote(v_all.at[ka], v_all.at[ka], v_send.at[0], v_recv.at[0], (pb, partner))
    v_pass = remote(v_all.at[across], v_all.at[across], v_send.at[2], v_recv.at[2], (pb, partner))
    own_w.wait()
    copies = ring(0)
    copies[0].start()
    copies[1].start()
    v_across.start()
    v_partner.start()
    x_copies = [
        remote(x_all.at[ka, pb], x_all.at[ka, pb], x_send.at[d - 1], x_recv.at[d - 1], ((pb + d) % n, ka)) for d in range(1, n)
    ]
    for copy in x_copies:
        copy.start()

    def k_copy(q, d):
        to = (ka + d) % parts
        return remote(
            k_part.at[q, :, pl.ds(pl.multiple_of(to * rows, rows), rows), :],
            k_in.at[d - 1, q],
            k_send.at[q, d - 1], k_recv.at[q, d - 1], (pb, to),
        )

    def block(k, carry):
        at = (place + n + ((k + 1) // 2) * (2 * (k % 2) - 1)) % n
        q = ring_index(at, n)
        high, low = halves(w_all[at])
        for s in range(capacity):
            p = source_ref[q * capacity + s]
            g_high[pl.ds(s * parts * rows, parts * rows), :] = v_high[p]
            g_low[pl.ds(s * parts * rows, parts * rows), :] = v_low[p]
        screened = dot_nt(g_high[...], high) + (dot_nt(g_high[...], low) + dot_nt(g_low[...], high))
        s_high, s_low = halves(screened)
        for s in range(capacity):
            span = slice(s * parts * rows, (s + 1) * parts * rows)
            conduct = c_ref[source_ref[q * capacity + s]]
            k_part[q, s] = dot_nt(s_high[span], conduct) + dot_nt(s_low[span], conduct)
        for d in range(1, parts):
            k_copy(q, d).start()
        return carry

    for step in range(1, n // 2):
        later = ring(step)
        copies[0].wait_recv()
        later[0].start()
        copies[1].wait_recv()
        later[1].start()
        copies[0].wait_send()
        copies[1].wait_send()
        copies = later
        if step == 1:
            for copy in x_copies:
                copy.wait()
            xk_copies = [
                remote(x_all.at[ka], x_all.at[ka], xk_send.at[d - 1], xk_recv.at[d - 1], (pb, (ka + d) % parts))
                for d in range(1, parts)
            ]
            for copy in xk_copies:
                copy.start()
        if step == n // 2 - 2:
            v_across.wait()
            v_pass.start()
            v_partner.wait()
            for copy in xk_copies:
                copy.wait()
            xout_ref[...] = x_all[...]
            v_pass.wait()

            def split(p, carry):
                for j in range(parts):
                    high, low = halves(v_all[j, p])
                    v_high[p, pl.ds(j * rows, rows), :] = high
                    v_low[p, pl.ds(j * rows, rows), :] = low
                return carry

            lax.fori_loop(0, pairs, split, 0)
            lax.fori_loop(0, n - 3, block, 0)
        if step == n // 2 - 1:
            lax.fori_loop(n - 3, n - 1, block, 0)
    copies[0].wait()
    copies[1].wait()
    lax.fori_loop(n - 1, n, block, 0)

    mine = pl.ds(pl.multiple_of(ka * rows, rows), rows)

    def total(q, carry):
        for d in range(1, parts):
            k_copy(q, d).wait()
        for s in range(capacity):
            value = k_part[q, s, mine, :]
            for d in range(1, parts):
                value = value + k_in[d - 1, q, s]
            k_ref[q, s] = value
        return carry

    lax.fori_loop(0, n, total, 0)


def reduce_kernel(n, parts, y_ref, out_ref, landed, send_sem, recv_sem):
    pb, ka = lax.axis_index("pb"), lax.axis_index("ka")
    count = n * parts
    me = pb * parts + ka
    barrier = pltpu.get_barrier_semaphore()

    def greet(d, carry):
        to = (me + d) % count
        pl.semaphore_signal(barrier, inc=1, device_id=(to // parts, to % parts), device_id_type=MESH)
        return carry

    lax.fori_loop(1, count, greet, 0)
    pl.semaphore_wait(barrier, count - 1)

    def copy(d):
        to = (me + d) % count
        return pltpu.make_async_remote_copy(
            src_ref=y_ref.at[to], dst_ref=landed.at[d], send_sem=send_sem.at[d], recv_sem=recv_sem.at[d],
            device_id=(to // parts, to % parts), device_id_type=MESH,
        )

    def send(d, carry):
        copy(d).start()
        return carry

    lax.fori_loop(1, count, send, 0)

    def take(d, total):
        copy(d).wait()
        return total + landed[d]

    out_ref[...] = lax.fori_loop(1, count, take, y_ref[me])


def ringed(valence, conduction, screened, momentum, kpairs, kpoint_slot, trial_blocks):
    high = lax.Precision.HIGH
    pair_dev, rows, waves = valence.shape
    n, parts = lax.axis_size("pb"), lax.axis_size("ka")
    capacity, slot_count, position, source = slots(momentum, pair_dev, n)
    trials = trial_blocks.shape[1] // (VB * CB)
    wide = VB * CB
    depth = conduction.shape[2]
    columns = conduction.shape[1]
    vmem = pl.BlockSpec(memory_space=pltpu.VMEM)
    any_space = pl.BlockSpec(memory_space=pl.ANY)
    dma = pltpu.SemaphoreType.DMA
    kernel, x_all = pl.pallas_call(
        functools.partial(kernel_blocks_kernel, n, parts, capacity),
        out_shape=(
            jax.ShapeDtypeStruct((n, capacity, rows, columns), jnp.float32),
            jax.ShapeDtypeStruct((parts, n, trials, wide), jnp.float32),
        ),
        in_specs=[pl.BlockSpec(memory_space=pltpu.SMEM), any_space, vmem, any_space, vmem],
        out_specs=(vmem, vmem),
        scratch_shapes=[
            pltpu.VMEM((n, depth, waves), jnp.float32),
            pltpu.VMEM((parts, pair_dev, rows, waves), jnp.float32),
            pltpu.VMEM((pair_dev, parts * rows, waves), jnp.bfloat16),
            pltpu.VMEM((pair_dev, parts * rows, waves), jnp.bfloat16),
            pltpu.VMEM((capacity * parts * rows, waves), jnp.bfloat16),
            pltpu.VMEM((capacity * parts * rows, waves), jnp.bfloat16),
            pltpu.VMEM((n, capacity, parts * rows, columns), jnp.float32),
            pltpu.VMEM((parts - 1, n, capacity, rows, columns), jnp.float32),
            pltpu.VMEM((parts, n, trials, wide), jnp.float32),
            dma((2,)), dma((3,)), dma((3,)), dma((n // 2, 2)), dma((n // 2, 2)),
            dma((n, parts - 1)), dma((n, parts - 1)), dma((n - 1,)), dma((n - 1,)), dma((parts - 1,)), dma((parts - 1,)),
        ],
        compiler_params=pltpu.CompilerParams(collective_id=0, has_side_effects=True, vmem_limit_bytes=56 * 1024 * 1024),
    )(source, valence, conduction, screened, trial_blocks.reshape(trials, wide))
    ka = lax.axis_index("ka")
    local_v = rows // VB
    mine = jnp.take(kernel.reshape(slot_count, rows, columns), position, axis=0)
    mixed = mine.reshape(pair_dev, local_v, VB, CB, CB).transpose(0, 1, 3, 2, 4).reshape(pair_dev, local_v * CB, wide)
    blocks = x_all.transpose(1, 0, 2, 3).reshape(n, parts * trials, wide)
    slot_near = jnp.take(kpoint_slot, kpairs[:, 0])
    slot_far = jnp.take(kpoint_slot, kpairs[:, 1])
    part = lax.dynamic_slice_in_dim(blocks, ka * local_v * CB, local_v * CB, axis=2)
    far_trials = jnp.take(blocks, slot_far, axis=0)
    near_trials = jnp.take(part, slot_near, axis=0)
    direct = jnp.einsum("pam,pnm->pna", mixed, far_trials, precision=high, preferred_element_type=jnp.float32)
    mirror = jnp.einsum("pam,pna->pnm", mixed, near_trials, precision=high, preferred_element_type=jnp.float32)
    kpoint_rows = jnp.arange(n, dtype=jnp.int32)[:, None]
    onehot_near = (slot_near[None, :] == kpoint_rows).astype(jnp.float32)
    onehot_far = (slot_far[None, :] == kpoint_rows).astype(jnp.float32)
    summed_near = jnp.einsum("kp,pna->kna", onehot_near, direct, precision=high, preferred_element_type=jnp.float32)
    summed_far = jnp.einsum("kp,pnm->knm", onehot_far, mirror, precision=high, preferred_element_type=jnp.float32)
    spread = lax.dynamic_update_slice_in_dim(jnp.zeros_like(summed_far), summed_near, ka * local_v * CB, axis=2)
    contributions = (summed_far + spread).reshape(n * parts, trials, wide)
    return reduced(n, parts, contributions).reshape(1, trials * wide)


def reduced(n, parts, contributions):
    count, trials, wide = contributions.shape
    vmem = pl.BlockSpec(memory_space=pltpu.VMEM)
    return pl.pallas_call(
        functools.partial(reduce_kernel, n, parts),
        out_shape=jax.ShapeDtypeStruct((trials, wide), jnp.float32),
        in_specs=[vmem],
        out_specs=vmem,
        scratch_shapes=[
            pltpu.VMEM((count, trials, wide), jnp.float32),
            pltpu.SemaphoreType.DMA((count,)),
            pltpu.SemaphoreType.DMA((count,)),
        ],
        compiler_params=pltpu.CompilerParams(collective_id=1, has_side_effects=True, vmem_limit_bytes=32 * 1024 * 1024),
    )(contributions)


def slots(momentum, pair_dev, owners):
    capacity = max(2, 2 * pair_dev // owners)
    slot_count = owners * capacity
    target = momentum[:, 0]
    indices = jnp.arange(pair_dev, dtype=jnp.int32)
    earlier = (target[:, None] == target[None, :]) & (indices[None, :] < indices[:, None])
    position = target * capacity + jnp.sum(earlier.astype(jnp.int32), axis=1)
    matches = position[None, :] == jnp.arange(slot_count, dtype=jnp.int32)[:, None]
    source = jnp.sum(jnp.where(matches, indices[None, :], 0), axis=1)
    return capacity, slot_count, position, source


def local(valence, conduction, screened, momentum, kpairs, kpoint_slot, trial_blocks):
    n, parts = lax.axis_size("pb"), lax.axis_size("ka")
    if n >= 8 and n % 2 == 0 and parts == 4 and n * conduction.shape[2] * valence.shape[2] * 4 <= 16 * 1024 * 1024:
        return ringed(valence, conduction, screened, momentum, kpairs, kpoint_slot, trial_blocks)
    return routed(valence, conduction, screened, momentum, kpairs, kpoint_slot, trial_blocks)


def routed(valence, conduction, screened, momentum, kpairs, kpoint_slot, trial_blocks):
    highest = lax.Precision.HIGHEST
    pair_dev = valence.shape[0]
    owners = lax.axis_size("pb")
    capacity = max(2, 2 * pair_dev // owners)
    slot_count = owners * capacity
    target = momentum[:, 0]
    indices = jnp.arange(pair_dev, dtype=jnp.int32)
    earlier = (target[:, None] == target[None, :]) & (indices[None, :] < indices[:, None])
    position = target * capacity + jnp.sum(earlier.astype(jnp.int32), axis=1)
    matches = position[None, :] == jnp.arange(slot_count, dtype=jnp.int32)[:, None]
    source = jnp.sum(jnp.where(matches, indices[None, :], 0), axis=1)
    filled = jnp.any(matches, axis=1)
    outgoing = jnp.where(filled[:, None, None], jnp.take(valence, source, axis=0), 0.0)
    outgoing = outgoing.reshape(owners, capacity, valence.shape[1], valence.shape[2])
    matrix = screened[0]
    product = jnp.einsum(
        "scrg,gh->scrh",
        lax.all_to_all(outgoing, "pb", split_axis=0, concat_axis=0, tiled=True),
        matrix,
        precision=highest,
        preferred_element_type=jnp.float32,
    )
    returned = lax.all_to_all(product, "pb", split_axis=0, concat_axis=0, tiled=True)
    by_slot = returned.reshape(slot_count, returned.shape[2], returned.shape[3])
    rows_back = jnp.take(by_slot, position, axis=0)
    columns = lax.all_to_all(rows_back, "ka", split_axis=2, concat_axis=1, tiled=True)
    conduct_wide = conduction.astype(jnp.float32)
    partial_kernel = jnp.einsum(
        "prg,pbg->prb", columns, conduct_wide, precision=highest, preferred_element_type=jnp.float32
    )
    kernel = lax.psum(partial_kernel, "ka")
    gathered = lax.all_gather(trial_blocks, "pb", axis=0, tiled=True)
    kpoint_count = gathered.shape[0]
    local_trials = gathered.shape[1] // (VB * CB)
    blocks = gathered.reshape(kpoint_count, local_trials, VB, CB)
    slot_near = jnp.take(kpoint_slot, kpairs[:, 0])
    slot_far = jnp.take(kpoint_slot, kpairs[:, 1])
    near_trials = jnp.take(blocks, slot_near, axis=0)
    far_trials = jnp.take(blocks, slot_far, axis=0)
    kernel_blocks = kernel.reshape(pair_dev, VB, VB, CB, CB)
    direct = jnp.einsum("pvwcd,pnwd->pnvc", kernel_blocks, far_trials, precision=highest)
    mirror = jnp.einsum("pvwcd,pnvc->pnwd", kernel_blocks, near_trials, precision=highest)
    kpoint_rows = jnp.arange(kpoint_count, dtype=jnp.int32)[:, None]
    onehot_near = (slot_near[None, :] == kpoint_rows).astype(jnp.float32)
    onehot_far = (slot_far[None, :] == kpoint_rows).astype(jnp.float32)
    summed = jnp.dot(
        onehot_near,
        direct.reshape(pair_dev, -1),
        precision=highest,
        preferred_element_type=jnp.float32,
    )
    summed = summed + jnp.dot(
        onehot_far,
        mirror.reshape(pair_dev, -1),
        precision=highest,
        preferred_element_type=jnp.float32,
    )
    return lax.psum_scatter(summed, "pb", scatter_dimension=0, tiled=True)


def solution(mesh):
    return jax.shard_map(
        local,
        mesh=mesh,
        in_specs=(
            P("pb", "ka", None),
            P("pb", None, "ka"),
            P("pb", None, None),
            P("pb", None),
            P("pb", None),
            P(),
            P("pb", "ka"),
        ),
        out_specs=P("pb", "ka"),
        check_vma=False,
    )
```

```python
import functools

import jax
import jax.numpy as jnp
from jax import lax
from jax.experimental import pallas as pl
from jax.experimental.pallas import tpu as pltpu
from jax.sharding import PartitionSpec as P

VB = 8
CB = 14
MESH = pl.DeviceIdType.MESH
NT = (((1,), (1,)), ((), ()))


def dot_nt(a, b):
    return lax.dot_general(a, b, NT, preferred_element_type=jnp.float32)


def halves(x):
    high = x.astype(jnp.bfloat16)
    return high, (x - high.astype(jnp.float32)).astype(jnp.bfloat16)


def ring_index(place, n):
    return jnp.where(place < n // 2, 2 * place, 2 * (n - 1 - place) + 1)


def kernel_blocks_kernel(
    n, parts, capacity,
    source_ref, v_ref, c_ref, w_ref, x_ref,
    k_ref, xout_ref,
    w_all, v_all, v_high, v_low, stacked, rows_of, k_part, k_in, x_all,
    local_sems, v_send, v_recv, ring_send, ring_recv, k_send, k_recv, x_send, x_recv, xk_send, xk_recv,
):
    pb, ka = lax.axis_index("pb"), lax.axis_index("ka")
    place = jnp.where(pb % 2 == 0, pb // 2, n - 1 - pb // 2)
    right = ring_index((place + 1) % n, n)
    left = ring_index((place + n - 1) % n, n)
    partner = ka + 1 - 2 * (ka % 2)
    across = (ka + 2) % parts
    rows = v_ref.shape[1]
    depth = w_all.shape[1]
    pairs = v_ref.shape[0]

    own_w = pltpu.make_async_copy(w_ref.at[0, pl.ds(pl.multiple_of(ka * depth, depth), depth), :], w_all.at[place], local_sems.at[0])
    own_v = pltpu.make_async_copy(v_ref, v_all.at[ka], local_sems.at[1])
    own_w.start()
    own_v.start()
    x_all[ka, pb] = x_ref[...]

    barrier = pltpu.get_barrier_semaphore()
    for d in range(1, n):
        pl.semaphore_signal(barrier, inc=1, device_id=((pb + d) % n, ka), device_id_type=MESH)
    for d in range(1, parts):
        pl.semaphore_signal(barrier, inc=1, device_id=(pb, (ka + d) % parts), device_id_type=MESH)
    pl.semaphore_wait(barrier, n + parts - 2)

    def remote(src, dst, send, recv, to):
        return pltpu.make_async_remote_copy(src_ref=src, dst_ref=dst, send_sem=send, recv_sem=recv, device_id=to, device_id_type=MESH)

    def ring(step):
        ahead = (place + n - step) % n
        behind = (place + step) % n
        if step < n // 2 - 1:
            go, back = w_all.at[ahead], w_all.at[behind]
        else:
            go = w_all.at[ahead, pl.ds(0, depth // 2)]
            back = w_all.at[behind, pl.ds(depth // 2, depth // 2)]
        return (
            remote(go, go, ring_send.at[step, 0], ring_recv.at[step, 0], (right, ka)),
            remote(back, back, ring_send.at[step, 1], ring_recv.at[step, 1], (left, ka)),
        )

    own_v.wait()
    v_across = remote(v_all.at[ka], v_all.at[ka], v_send.at[1], v_recv.at[1], (pb, across))
    v_partner = remote(v_all.at[ka], v_all.at[ka], v_send.at[0], v_recv.at[0], (pb, partner))
    v_pass = remote(v_all.at[across], v_all.at[across], v_send.at[2], v_recv.at[2], (pb, partner))
    own_w.wait()
    copies = ring(0)
    copies[0].start()
    copies[1].start()
    v_across.start()
    v_partner.start()
    x_copies = [
        remote(x_all.at[ka, pb], x_all.at[ka, pb], x_send.at[d - 1], x_recv.at[d - 1], ((pb + d) % n, ka)) for d in range(1, n)
    ]
    for copy in x_copies:
        copy.start()

    two = 2 * rows
    span = capacity * two
    chip = ka - ka % 2
    other = (chip + 2) % parts

    def split(side):
        base = chip if side == 0 else other

        def one(p, carry):
            for j in range(2):
                high, low = halves(v_all[base + j, p])
                v_high[side, p, pl.ds(j * rows, rows), :] = high
                v_low[side, p, pl.ds(j * rows, rows), :] = low
            return carry

        lax.fori_loop(0, pairs, one, 0)

    def k_copy(q, d):
        if d == 0:
            to, at = partner, (1 - ka % 2) * rows
        elif d == 1:
            to, at = across, two + (ka % 2) * rows
        else:
            to, at = (partner + 2) % parts, two + (1 - ka % 2) * rows
        return remote(
            k_part.at[q, :, pl.ds(pl.multiple_of(at, rows), rows), :], k_in.at[d, q], k_send.at[q, d], k_recv.at[q, d], (pb, to)
        )

    def place_of(k):
        return (place + n + ((k + 1) // 2) * (2 * (k % 2) - 1)) % n

    def screen(side, first, last):
        def block(k, carry):
            at = place_of(k)
            q = ring_index(at, n)
            high, low = halves(w_all[at])
            for s in range(capacity):
                p = source_ref[q * capacity + s]
                stacked[pl.ds(s * two, two), :] = v_high[side, p]
                stacked[pl.ds(span + s * two, two), :] = v_low[side, p]
            both = dot_nt(stacked[...], high)
            screened = both[:span] + (both[span:] + dot_nt(stacked[pl.ds(0, span), :], low))
            s_high, s_low = halves(screened)
            for s in range(capacity):
                rows_of[at, s, pl.ds(side * two, two), :] = s_high[s * two:(s + 1) * two]
                rows_of[at, s, pl.ds(2 * two + side * two, two), :] = s_low[s * two:(s + 1) * two]
            if side == 1:
                for s in range(capacity):
                    both = dot_nt(rows_of[at, s], c_ref[source_ref[q * capacity + s]])
                    k_part[q, s] = both[:2 * two] + both[2 * two:]
                for d in range(parts - 1):
                    k_copy(q, d).start()
            return carry

        lax.fori_loop(first, last, block, 0)

    v_partner.wait()
    split(0)
    screen(0, 0, 1)
    for step in range(1, n // 2):
        later = ring(step)
        copies[0].wait_recv()
        later[0].start()
        copies[1].wait_recv()
        later[1].start()
        copies[0].wait_send()
        copies[1].wait_send()
        copies = later
        if step == 1:
            for copy in x_copies:
                copy.wait()
            xk_copies = [
                remote(x_all.at[ka], x_all.at[ka], xk_send.at[d - 1], xk_recv.at[d - 1], (pb, (ka + d) % parts))
                for d in range(1, parts)
            ]
            for copy in xk_copies:
                copy.start()
        if step < n // 2 - 2:
            screen(0, 2 * step - 1, 2 * step + 1)
        if step == n // 2 - 3:
            v_across.wait()
            v_pass.start()
        if step == n // 2 - 2:
            v_pass.wait()
            split(1)
            screen(1, 0, n - 5)
            screen(0, n - 5, n - 3)
            for copy in xk_copies:
                copy.wait()
            xout_ref[...] = x_all[...]
        if step == n // 2 - 1:
            screen(1, n - 5, n - 3)
            screen(0, n - 3, n - 1)
            screen(1, n - 3, n - 1)
    copies[0].wait()
    copies[1].wait()
    screen(0, n - 1, n)
    screen(1, n - 1, n)

    mine = pl.ds(pl.multiple_of((ka % 2) * rows, rows), rows)

    def total(q, carry):
        for d in range(parts - 1):
            k_copy(q, d).wait()
        for s in range(capacity):
            k_ref[q, s] = k_part[q, s, mine, :] + (k_in[0, q, s] + (k_in[1, q, s] + k_in[2, q, s]))
        return carry

    lax.fori_loop(0, n, total, 0)


def response_kernel(
    n, parts,
    position_ref, near_ref, far_ref, k_ref, x_ref, mask_ref, spread_ref, put_ref,
    out_ref,
    wide_rows, mixed, m_high, m_low, x_stack, x_part, direct, mirror, given, landed, joined, landed_pb,
    ka_send, ka_recv, pb_send, pb_recv,
):
    pb, ka = lax.axis_index("pb"), lax.axis_index("ka")
    pairs = direct.shape[0]
    trials, wide = out_ref.shape
    every = parts * trials
    band = put_ref.shape[0]
    local_v = k_ref.shape[1] // VB
    tall = band // local_v
    barrier = pltpu.get_barrier_semaphore()
    for d in range(1, n):
        pl.semaphore_signal(barrier, inc=1, device_id=((pb + d) % n, ka), device_id_type=MESH)
    for d in range(1, parts):
        pl.semaphore_signal(barrier, inc=1, device_id=(pb, (ka + d) % parts), device_id_type=MESH)

    def dot(a, b):
        return jnp.dot(a, b, preferred_element_type=jnp.float32)

    for w in range(VB):
        def fill(p, carry):
            values = k_ref[position_ref[p]]
            for v in range(local_v):
                row = values[v * VB + w:v * VB + w + 1]
                high, low = halves(jnp.broadcast_to(row, mask_ref.shape) * mask_ref[...])
                wide_rows[0, p, pl.ds(v * tall, tall), :] = high
                wide_rows[1, p, pl.ds(v * tall, tall), :] = low
            return carry

        lax.fori_loop(0, pairs, fill, 0)
        lanes = wide_rows.shape[-1]
        part = dot(wide_rows[...].reshape(2 * pairs * band, lanes), spread_ref[w])
        if w == 0:
            mixed[...] = part
        else:
            mixed[...] += part

    def cut(p, carry):
        value = mixed[pl.ds(pl.multiple_of(p * band, band), band), :]
        value = value + mixed[pl.ds(pl.multiple_of((pairs + p) * band, band), band), :]
        high, low = halves(value)
        m_high[p] = high
        m_low[p] = low
        return carry

    lax.fori_loop(0, pairs, cut, 0)

    def trial(m, carry):
        for j in range(parts):
            high, low = halves(x_ref[j, m])
            x_stack[m, pl.ds(j * trials, trials), :] = high
            x_stack[m, pl.ds(every + j * trials, trials), :] = low
        x_part[m] = dot_nt(x_stack[m], put_ref[...]).astype(jnp.bfloat16)
        return carry

    lax.fori_loop(0, n, trial, 0)

    def pair(p, carry):
        far = x_stack[far_ref[p]]
        both = dot_nt(far, m_high[p])
        direct[p] = both[:every] + (both[every:] + dot_nt(far[:every], m_low[p]))
        near = x_part[near_ref[p]]
        both = dot(near, m_high[p])
        mirror[p] = both[:every] + (both[every:] + dot(near[:every], m_low[p]))
        return carry

    lax.fori_loop(0, pairs, pair, 0)
    pl.semaphore_wait(barrier, n + parts - 2)

    def remote(src, dst, send, recv, to):
        return pltpu.make_async_remote_copy(src_ref=src, dst_ref=dst, send_sem=send, recv_sem=recv, device_id=to, device_id_type=MESH)

    def ka_copy(m, d):
        to = (ka + d) % parts
        return remote(given.at[m, to], landed.at[d - 1, m], ka_send.at[m, d - 1], ka_recv.at[m, d - 1], (pb, to))

    def pb_copy(d):
        to = (pb + d) % n
        return remote(joined.at[to], landed_pb.at[d - 1], pb_send.at[d - 1], pb_recv.at[d - 1], (to, ka))

    def gather(m, carry):
        def add(ref, index_ref):
            def step(p, total):
                return total + ref[p] * (index_ref[p] == m).astype(jnp.float32)

            return lax.fori_loop(0, pairs, step, jnp.zeros(ref.shape[1:], jnp.float32))

        high, low = halves(add(direct, near_ref))
        value = add(mirror, far_ref) + (dot(high, put_ref[...]) + dot(low, put_ref[...]))
        for j in range(parts):
            given[m, j] = value[j * trials:(j + 1) * trials]
        for d in range(1, parts):
            ka_copy(m, d).start()
        return carry

    lax.fori_loop(0, n, gather, 0)

    def join(m, carry):
        value = given[m, ka]
        for d in range(1, parts):
            ka_copy(m, d).wait()
            value = value + landed[d - 1, m]
        joined[m] = value
        return carry

    lax.fori_loop(0, n, join, 0)
    for d in range(1, n):
        pb_copy(d).start()
    value = joined[pb]
    for d in range(1, n):
        pb_copy(d).wait()
        value = value + landed_pb[d - 1]
    out_ref[...] = value


def ringed(valence, conduction, screened, momentum, kpairs, kpoint_slot, trial_blocks):
    pair_dev, rows, waves = valence.shape
    n, parts = lax.axis_size("pb"), lax.axis_size("ka")
    capacity, slot_count, position, source = slots(momentum, pair_dev, n)
    trials = trial_blocks.shape[1] // (VB * CB)
    wide = VB * CB
    depth = conduction.shape[2]
    columns = conduction.shape[1]
    vmem = pl.BlockSpec(memory_space=pltpu.VMEM)
    any_space = pl.BlockSpec(memory_space=pl.ANY)
    dma = pltpu.SemaphoreType.DMA
    kernel, x_all = pl.pallas_call(
        functools.partial(kernel_blocks_kernel, n, parts, capacity),
        out_shape=(
            jax.ShapeDtypeStruct((n, capacity, rows, columns), jnp.float32),
            jax.ShapeDtypeStruct((parts, n, trials, wide), jnp.float32),
        ),
        in_specs=[pl.BlockSpec(memory_space=pltpu.SMEM), any_space, vmem, any_space, vmem],
        out_specs=(vmem, vmem),
        scratch_shapes=[
            pltpu.VMEM((n, depth, waves), jnp.float32),
            pltpu.VMEM((parts, pair_dev, rows, waves), jnp.float32),
            pltpu.VMEM((2, pair_dev, 2 * rows, waves), jnp.bfloat16),
            pltpu.VMEM((2, pair_dev, 2 * rows, waves), jnp.bfloat16),
            pltpu.VMEM((capacity * 4 * rows, waves), jnp.bfloat16),
            pltpu.VMEM((n, capacity, 8 * rows, depth), jnp.bfloat16),
            pltpu.VMEM((n, capacity, parts * rows, columns), jnp.float32),
            pltpu.VMEM((parts - 1, n, capacity, rows, columns), jnp.float32),
            pltpu.VMEM((parts, n, trials, wide), jnp.float32),
            dma((2,)), dma((3,)), dma((3,)), dma((n // 2, 2)), dma((n // 2, 2)),
            dma((n, parts - 1)), dma((n, parts - 1)), dma((n - 1,)), dma((n - 1,)), dma((parts - 1,)), dma((parts - 1,)),
        ],
        compiler_params=pltpu.CompilerParams(collective_id=0, has_side_effects=True, vmem_limit_bytes=56 * 1024 * 1024),
    )(source, valence, conduction, screened, trial_blocks.reshape(trials, wide))
    ka = lax.axis_index("ka")
    local_v = rows // VB
    tall = -(-CB // 16) * 16
    band = local_v * tall
    every = parts * trials
    c_of, d_of = jnp.arange(columns, dtype=jnp.int32) // CB, jnp.arange(columns, dtype=jnp.int32) % CB
    mask = (jnp.arange(tall, dtype=jnp.int32)[:, None] == c_of[None, :]).astype(jnp.float32)
    w_to, d_to = jnp.arange(wide, dtype=jnp.int32) // CB, jnp.arange(wide, dtype=jnp.int32) % CB
    same_d = d_of[:, None] == d_to[None, :]
    spread = (same_d[None] & (w_to[None, None, :] == jnp.arange(VB, dtype=jnp.int32)[:, None, None])).astype(jnp.bfloat16)
    v_row, c_row = jnp.arange(band, dtype=jnp.int32) // tall, jnp.arange(band, dtype=jnp.int32) % tall
    put = ((ka * local_v + v_row)[:, None] == w_to[None, :]) & (c_row[:, None] == d_to[None, :])
    smem = pl.BlockSpec(memory_space=pltpu.SMEM)
    result = pl.pallas_call(
        functools.partial(response_kernel, n, parts),
        out_shape=jax.ShapeDtypeStruct((trials, wide), jnp.float32),
        in_specs=[smem] * 3 + [vmem] * 5,
        out_specs=vmem,
        scratch_shapes=[
            pltpu.VMEM((2, pair_dev, band, columns), jnp.bfloat16),
            pltpu.VMEM((2 * pair_dev * band, wide), jnp.float32),
            pltpu.VMEM((pair_dev, band, wide), jnp.bfloat16),
            pltpu.VMEM((pair_dev, band, wide), jnp.bfloat16),
            pltpu.VMEM((n, 2 * every, wide), jnp.bfloat16),
            pltpu.VMEM((n, 2 * every, band), jnp.bfloat16),
            pltpu.VMEM((pair_dev, every, band), jnp.float32),
            pltpu.VMEM((pair_dev, every, wide), jnp.float32),
            pltpu.VMEM((n, parts, trials, wide), jnp.float32),
            pltpu.VMEM((parts - 1, n, trials, wide), jnp.float32),
            pltpu.VMEM((n, trials, wide), jnp.float32),
            pltpu.VMEM((n - 1, trials, wide), jnp.float32),
            dma((n, parts - 1)), dma((n, parts - 1)), dma((n - 1,)), dma((n - 1,)),
        ],
        compiler_params=pltpu.CompilerParams(collective_id=1, has_side_effects=True, vmem_limit_bytes=48 * 1024 * 1024),
    )(
        position, jnp.take(kpoint_slot, kpairs[:, 0]), jnp.take(kpoint_slot, kpairs[:, 1]),
        kernel.reshape(slot_count, rows, columns), x_all, mask, spread, put.astype(jnp.bfloat16),
    )
    return result.reshape(1, trials * wide)


def slots(momentum, pair_dev, owners):
    capacity = max(2, 2 * pair_dev // owners)
    slot_count = owners * capacity
    target = momentum[:, 0]
    indices = jnp.arange(pair_dev, dtype=jnp.int32)
    earlier = (target[:, None] == target[None, :]) & (indices[None, :] < indices[:, None])
    position = target * capacity + jnp.sum(earlier.astype(jnp.int32), axis=1)
    matches = position[None, :] == jnp.arange(slot_count, dtype=jnp.int32)[:, None]
    source = jnp.sum(jnp.where(matches, indices[None, :], 0), axis=1)
    return capacity, slot_count, position, source


def local(valence, conduction, screened, momentum, kpairs, kpoint_slot, trial_blocks):
    n, parts = lax.axis_size("pb"), lax.axis_size("ka")
    if n >= 8 and n % 2 == 0 and parts == 4 and n * conduction.shape[2] * valence.shape[2] * 4 <= 16 * 1024 * 1024:
        return ringed(valence, conduction, screened, momentum, kpairs, kpoint_slot, trial_blocks)
    return routed(valence, conduction, screened, momentum, kpairs, kpoint_slot, trial_blocks)


def routed(valence, conduction, screened, momentum, kpairs, kpoint_slot, trial_blocks):
    highest = lax.Precision.HIGHEST
    pair_dev = valence.shape[0]
    owners = lax.axis_size("pb")
    capacity = max(2, 2 * pair_dev // owners)
    slot_count = owners * capacity
    target = momentum[:, 0]
    indices = jnp.arange(pair_dev, dtype=jnp.int32)
    earlier = (target[:, None] == target[None, :]) & (indices[None, :] < indices[:, None])
    position = target * capacity + jnp.sum(earlier.astype(jnp.int32), axis=1)
    matches = position[None, :] == jnp.arange(slot_count, dtype=jnp.int32)[:, None]
    source = jnp.sum(jnp.where(matches, indices[None, :], 0), axis=1)
    filled = jnp.any(matches, axis=1)
    outgoing = jnp.where(filled[:, None, None], jnp.take(valence, source, axis=0), 0.0)
    outgoing = outgoing.reshape(owners, capacity, valence.shape[1], valence.shape[2])
    matrix = screened[0]
    product = jnp.einsum(
        "scrg,gh->scrh",
        lax.all_to_all(outgoing, "pb", split_axis=0, concat_axis=0, tiled=True),
        matrix,
        precision=highest,
        preferred_element_type=jnp.float32,
    )
    returned = lax.all_to_all(product, "pb", split_axis=0, concat_axis=0, tiled=True)
    by_slot = returned.reshape(slot_count, returned.shape[2], returned.shape[3])
    rows_back = jnp.take(by_slot, position, axis=0)
    columns = lax.all_to_all(rows_back, "ka", split_axis=2, concat_axis=1, tiled=True)
    conduct_wide = conduction.astype(jnp.float32)
    partial_kernel = jnp.einsum(
        "prg,pbg->prb", columns, conduct_wide, precision=highest, preferred_element_type=jnp.float32
    )
    kernel = lax.psum(partial_kernel, "ka")
    gathered = lax.all_gather(trial_blocks, "pb", axis=0, tiled=True)
    kpoint_count = gathered.shape[0]
    local_trials = gathered.shape[1] // (VB * CB)
    blocks = gathered.reshape(kpoint_count, local_trials, VB, CB)
    slot_near = jnp.take(kpoint_slot, kpairs[:, 0])
    slot_far = jnp.take(kpoint_slot, kpairs[:, 1])
    near_trials = jnp.take(blocks, slot_near, axis=0)
    far_trials = jnp.take(blocks, slot_far, axis=0)
    kernel_blocks = kernel.reshape(pair_dev, VB, VB, CB, CB)
    direct = jnp.einsum("pvwcd,pnwd->pnvc", kernel_blocks, far_trials, precision=highest)
    mirror = jnp.einsum("pvwcd,pnvc->pnwd", kernel_blocks, near_trials, precision=highest)
    kpoint_rows = jnp.arange(kpoint_count, dtype=jnp.int32)[:, None]
    onehot_near = (slot_near[None, :] == kpoint_rows).astype(jnp.float32)
    onehot_far = (slot_far[None, :] == kpoint_rows).astype(jnp.float32)
    summed = jnp.dot(
        onehot_near,
        direct.reshape(pair_dev, -1),
        precision=highest,
        preferred_element_type=jnp.float32,
    )
    summed = summed + jnp.dot(
        onehot_far,
        mirror.reshape(pair_dev, -1),
        precision=highest,
        preferred_element_type=jnp.float32,
    )
    return lax.psum_scatter(summed, "pb", scatter_dimension=0, tiled=True)


def solution(mesh):
    return jax.shard_map(
        local,
        mesh=mesh,
        in_specs=(
            P("pb", "ka", None),
            P("pb", None, "ka"),
            P("pb", None, None),
            P("pb", None),
            P("pb", None),
            P(),
            P("pb", "ka"),
        ),
        out_specs=P("pb", "ka"),
        check_vma=False,
    )
```

```python
import functools

import jax
import jax.numpy as jnp
import numpy as np
from jax import lax
from jax.experimental import pallas as pl
from jax.experimental.pallas import tpu as pltpu
from jax.sharding import PartitionSpec as P

VB = 8
CB = 14
MESH = pl.DeviceIdType.MESH
NT = (((1,), (1,)), ((), ()))


def dot_nt(a, b):
    return lax.dot_general(a, b, NT, preferred_element_type=jnp.float32)


def halves(x):
    high = x.astype(jnp.bfloat16)
    return high, (x - high.astype(jnp.float32)).astype(jnp.bfloat16)


def ring_index(place, n):
    return jnp.where(place < n // 2, 2 * place, 2 * (n - 1 - place) + 1)


def kernel_blocks_kernel(
    n, parts, capacity,
    source_ref, v_ref, c_ref, w_ref, x_ref,
    k_ref, xout_ref,
    w_all, v_all, v_high, v_low, stacked, rows_of, k_part, k_in, x_all,
    local_sems, v_send, v_recv, ring_send, ring_recv, k_send, k_recv, x_send, x_recv, xk_send, xk_recv,
):
    pb, ka = lax.axis_index("pb"), lax.axis_index("ka")
    place = jnp.where(pb % 2 == 0, pb // 2, n - 1 - pb // 2)
    right = ring_index((place + 1) % n, n)
    left = ring_index((place + n - 1) % n, n)
    partner = ka + 1 - 2 * (ka % 2)
    across = (ka + 2) % parts
    rows = v_ref.shape[1]
    depth = w_all.shape[1]
    pairs = v_ref.shape[0]

    own_w = pltpu.make_async_copy(w_ref.at[0, pl.ds(pl.multiple_of(ka * depth, depth), depth), :], w_all.at[place], local_sems.at[0])
    own_v = pltpu.make_async_copy(v_ref, v_all.at[ka], local_sems.at[1])
    own_w.start()
    own_v.start()
    x_all[ka, pb] = x_ref[...]

    barrier = pltpu.get_barrier_semaphore()
    for d in range(1, n):
        pl.semaphore_signal(barrier, inc=1, device_id=((pb + d) % n, ka), device_id_type=MESH)
    for d in range(1, parts):
        pl.semaphore_signal(barrier, inc=1, device_id=(pb, (ka + d) % parts), device_id_type=MESH)
    pl.semaphore_wait(barrier, n + parts - 2)

    def remote(src, dst, send, recv, to):
        return pltpu.make_async_remote_copy(src_ref=src, dst_ref=dst, send_sem=send, recv_sem=recv, device_id=to, device_id_type=MESH)

    def ring(step):
        ahead = (place + n - step) % n
        behind = (place + step) % n
        if step < n // 2 - 1:
            go, back = w_all.at[ahead], w_all.at[behind]
        else:
            go = w_all.at[ahead, pl.ds(0, depth // 2)]
            back = w_all.at[behind, pl.ds(depth // 2, depth // 2)]
        return (
            remote(go, go, ring_send.at[step, 0], ring_recv.at[step, 0], (right, ka)),
            remote(back, back, ring_send.at[step, 1], ring_recv.at[step, 1], (left, ka)),
        )

    own_v.wait()
    v_across = remote(v_all.at[ka], v_all.at[ka], v_send.at[1], v_recv.at[1], (pb, across))
    v_partner = remote(v_all.at[ka], v_all.at[ka], v_send.at[0], v_recv.at[0], (pb, partner))
    v_pass = remote(v_all.at[across], v_all.at[across], v_send.at[2], v_recv.at[2], (pb, partner))
    own_w.wait()
    copies = ring(0)
    copies[0].start()
    copies[1].start()
    v_across.start()
    v_partner.start()
    x_copies = [
        remote(x_all.at[ka, pb], x_all.at[ka, pb], x_send.at[d - 1], x_recv.at[d - 1], ((pb + d) % n, ka)) for d in range(1, n)
    ]
    for copy in x_copies:
        copy.start()

    two = 2 * rows
    span = capacity * two
    chip = ka - ka % 2
    other = (chip + 2) % parts

    def split(side):
        base = chip if side == 0 else other

        def one(p, carry):
            for j in range(2):
                high, low = halves(v_all[base + j, p])
                v_high[side, p, pl.ds(j * rows, rows), :] = high
                v_low[side, p, pl.ds(j * rows, rows), :] = low
            return carry

        lax.fori_loop(0, pairs, one, 0)

    def k_copy(q, d):
        if d == 0:
            to, at = partner, (1 - ka % 2) * rows
        elif d == 1:
            to, at = across, two + (ka % 2) * rows
        else:
            to, at = (partner + 2) % parts, two + (1 - ka % 2) * rows
        return remote(
            k_part.at[q, :, pl.ds(pl.multiple_of(at, rows), rows), :], k_in.at[d, q], k_send.at[q, d], k_recv.at[q, d], (pb, to)
        )

    def place_of(k):
        return (place + n + ((k + 1) // 2) * (2 * (k % 2) - 1)) % n

    def screen(side, first, last):
        def block(k, carry):
            at = place_of(k)
            q = ring_index(at, n)
            high, low = halves(w_all[at])
            for s in range(capacity):
                p = source_ref[q * capacity + s]
                stacked[pl.ds(s * two, two), :] = v_high[side, p]
                stacked[pl.ds(span + s * two, two), :] = v_low[side, p]
            both = dot_nt(stacked[...], high)
            screened = both[:span] + (both[span:] + dot_nt(stacked[pl.ds(0, span), :], low))
            s_high, s_low = halves(screened)
            for s in range(capacity):
                rows_of[at, s, pl.ds(side * two, two), :] = s_high[s * two:(s + 1) * two]
                rows_of[at, s, pl.ds(2 * two + side * two, two), :] = s_low[s * two:(s + 1) * two]
            if side == 1:
                for s in range(capacity):
                    both = dot_nt(rows_of[at, s], c_ref[source_ref[q * capacity + s]])
                    k_part[q, s] = both[:2 * two] + both[2 * two:]
                for d in range(parts - 1):
                    k_copy(q, d).start()
            return carry

        lax.fori_loop(first, last, block, 0)

    v_partner.wait()
    split(0)
    screen(0, 0, 1)
    for step in range(1, n // 2):
        later = ring(step)
        copies[0].wait_recv()
        later[0].start()
        copies[1].wait_recv()
        later[1].start()
        copies[0].wait_send()
        copies[1].wait_send()
        copies = later
        if step == 1:
            for copy in x_copies:
                copy.wait()
            xk_copies = [
                remote(x_all.at[ka], x_all.at[ka], xk_send.at[d - 1], xk_recv.at[d - 1], (pb, (ka + d) % parts))
                for d in range(1, parts)
            ]
            for copy in xk_copies:
                copy.start()
        if step < n // 2 - 2:
            screen(0, 2 * step - 1, 2 * step + 1)
        if step == n // 2 - 3:
            v_across.wait()
            v_pass.start()
        if step == n // 2 - 2:
            v_pass.wait()
            split(1)
            screen(1, 0, n - 5)
            screen(0, n - 5, n - 3)
            for copy in xk_copies:
                copy.wait()
            xout_ref[...] = x_all[...]
        if step == n // 2 - 1:
            screen(1, n - 5, n - 3)
            screen(0, n - 3, n - 1)
            screen(1, n - 3, n - 1)
    copies[0].wait()
    copies[1].wait()
    screen(0, n - 1, n)
    screen(1, n - 1, n)

    mine = pl.ds(pl.multiple_of((ka % 2) * rows, rows), rows)

    def total(q, carry):
        for d in range(parts - 1):
            k_copy(q, d).wait()
        for s in range(capacity):
            k_ref[q, s] = k_part[q, s, mine, :] + (k_in[0, q, s] + (k_in[1, q, s] + k_in[2, q, s]))
        return carry

    lax.fori_loop(0, n, total, 0)


def response_kernel(
    n, parts,
    position_ref, far_ref, k_ref, x_ref, mask_ref, spread_ref, near_ref, pick_ref,
    out_ref,
    wide_rows, mixed, by_far, x_high, x_low, given, landed, joined, landed_pb,
    ka_send, ka_recv, pb_send, pb_recv,
):
    pb, ka = lax.axis_index("pb"), lax.axis_index("ka")
    trials, wide = x_ref.shape[2:]
    full = spread_ref.shape[2]
    tall = mask_ref.shape[0]
    local_v = k_ref.shape[1] // VB
    band = local_v * tall
    pairs = position_ref.shape[0]
    barrier = pltpu.get_barrier_semaphore()
    for d in range(1, n):
        pl.semaphore_signal(barrier, inc=1, device_id=((pb + d) % n, ka), device_id_type=MESH)
    for d in range(1, parts):
        pl.semaphore_signal(barrier, inc=1, device_id=(pb, (ka + d) % parts), device_id_type=MESH)

    def dot(a, b):
        return jnp.dot(a, b, preferred_element_type=jnp.float32)

    x_high[...] = jnp.zeros_like(x_high)
    x_low[...] = jnp.zeros_like(x_low)
    for m in range(n):
        for j in range(parts):
            high, low = halves(x_ref[j, m])
            x_high[pl.ds(j * trials, trials), pl.ds(m * full, wide)] = high
            x_low[pl.ds(j * trials, trials), pl.ds(m * full, wide)] = low

    def fill(p, carry):
        values = k_ref[position_ref[p]]
        for w in range(VB):
            for v in range(local_v):
                row = values[v * VB + w:v * VB + w + 1]
                high, low = halves(jnp.broadcast_to(row, mask_ref.shape) * mask_ref[...])
                wide_rows[w, p, pl.ds(v * tall, tall), :] = high
                wide_rows[w, pairs + p, pl.ds(v * tall, tall), :] = low
        return carry

    lax.fori_loop(0, pairs, fill, 0)
    lanes = wide_rows.shape[-1]
    for w in range(VB):
        part = dot(wide_rows[w].reshape(2 * pairs * band, lanes), spread_ref[w])
        if w == 0:
            mixed[...] = part
        else:
            mixed[...] += part

    def cut(p, carry):
        at = pl.multiple_of(p * band, band)
        value = mixed[pl.ds(at, band), :] + mixed[pl.ds(pl.multiple_of((pairs + p) * band, band), band), :]
        for m in range(n):
            high, low = halves(value * (far_ref[p] == m).astype(jnp.float32))
            by_far[0, pl.ds(at, band), pl.ds(m * full, full)] = high
            by_far[1, pl.ds(at, band), pl.ds(m * full, full)] = low
        return carry

    lax.fori_loop(0, pairs, cut, 0)
    g_high, g_low = halves(dot(near_ref[...], by_far[0]) + dot(near_ref[...], by_far[1]))
    pick = pick_ref[...]
    p_high = dot_nt(x_high[...], pick).astype(jnp.bfloat16)
    p_low = dot_nt(x_low[...], pick).astype(jnp.bfloat16)
    direct = dot_nt(x_high[...], g_high) + (dot_nt(x_high[...], g_low) + dot_nt(x_low[...], g_high))
    d_high, d_low = halves(direct)
    value = dot(p_high, g_high) + (dot(p_high, g_low) + dot(p_low, g_high))
    value = value + (dot(d_high, pick) + dot(d_low, pick))
    for m in range(n):
        for j in range(parts):
            given[m, j] = value[j * trials:(j + 1) * trials, m * full:(m + 1) * full]
    pl.semaphore_wait(barrier, n + parts - 2)

    def remote(src, dst, send, recv, to):
        return pltpu.make_async_remote_copy(src_ref=src, dst_ref=dst, send_sem=send, recv_sem=recv, device_id=to, device_id_type=MESH)

    def ka_copy(m, d):
        to = (ka + d) % parts
        return remote(given.at[m, to], landed.at[d - 1, m], ka_send.at[m, d - 1], ka_recv.at[m, d - 1], (pb, to))

    def pb_copy(d):
        to = (pb + d) % n
        return remote(joined.at[to], landed_pb.at[d - 1], pb_send.at[d - 1], pb_recv.at[d - 1], (to, ka))

    def send(m, carry):
        for d in range(1, parts):
            ka_copy(m, d).start()
        return carry

    lax.fori_loop(0, n, send, 0)

    def join(m, carry):
        value = given[m, ka]
        for d in range(1, parts):
            ka_copy(m, d).wait()
            value = value + landed[d - 1, m]
        joined[m] = value
        return carry

    lax.fori_loop(0, n, join, 0)
    for d in range(1, n):
        pb_copy(d).start()
    value = joined[pb]
    for d in range(1, n):
        pb_copy(d).wait()
        value = value + landed_pb[d - 1]
    out_ref[...] = value[:, :wide]


def ringed(valence, conduction, screened, momentum, kpairs, kpoint_slot, trial_blocks):
    pair_dev, rows, waves = valence.shape
    n, parts = lax.axis_size("pb"), lax.axis_size("ka")
    capacity, slot_count, position, source = slots(momentum, pair_dev, n)
    trials = trial_blocks.shape[1] // (VB * CB)
    wide = VB * CB
    depth = conduction.shape[2]
    columns = conduction.shape[1]
    vmem = pl.BlockSpec(memory_space=pltpu.VMEM)
    any_space = pl.BlockSpec(memory_space=pl.ANY)
    dma = pltpu.SemaphoreType.DMA
    kernel, x_all = pl.pallas_call(
        functools.partial(kernel_blocks_kernel, n, parts, capacity),
        out_shape=(
            jax.ShapeDtypeStruct((n, capacity, rows, columns), jnp.float32),
            jax.ShapeDtypeStruct((parts, n, trials, wide), jnp.float32),
        ),
        in_specs=[pl.BlockSpec(memory_space=pltpu.SMEM), any_space, vmem, any_space, vmem],
        out_specs=(vmem, vmem),
        scratch_shapes=[
            pltpu.VMEM((n, depth, waves), jnp.float32),
            pltpu.VMEM((parts, pair_dev, rows, waves), jnp.float32),
            pltpu.VMEM((2, pair_dev, 2 * rows, waves), jnp.bfloat16),
            pltpu.VMEM((2, pair_dev, 2 * rows, waves), jnp.bfloat16),
            pltpu.VMEM((capacity * 4 * rows, waves), jnp.bfloat16),
            pltpu.VMEM((n, capacity, 8 * rows, depth), jnp.bfloat16),
            pltpu.VMEM((n, capacity, parts * rows, columns), jnp.float32),
            pltpu.VMEM((parts - 1, n, capacity, rows, columns), jnp.float32),
            pltpu.VMEM((parts, n, trials, wide), jnp.float32),
            dma((2,)), dma((3,)), dma((3,)), dma((n // 2, 2)), dma((n // 2, 2)),
            dma((n, parts - 1)), dma((n, parts - 1)), dma((n - 1,)), dma((n - 1,)), dma((parts - 1,)), dma((parts - 1,)),
        ],
        compiler_params=pltpu.CompilerParams(collective_id=0, has_side_effects=True, vmem_limit_bytes=56 * 1024 * 1024),
    )(source, valence, conduction, screened, trial_blocks.reshape(trials, wide))
    ka = lax.axis_index("ka")
    local_v = rows // VB
    tall = -(-CB // 16) * 16
    band = local_v * tall
    every = parts * trials
    full = -(-wide // 128) * 128
    c_of, d_of = np.arange(columns) // CB, np.arange(columns) % CB
    lane = np.arange(full)
    w_to, d_to = lane // CB, lane % CB
    mask = (np.arange(tall)[:, None] == c_of[None, :]).astype(np.float32)
    at_w = (w_to[None, None, :] == np.arange(VB)[:, None, None]) & (lane < wide)[None, None, :]
    spread = ((d_of[:, None] == d_to[None, :])[None] & at_w).astype(jnp.bfloat16)
    band_row = np.arange(n * band)
    k_row, v_row, c_row = band_row // band, band_row % band // tall, band_row % tall
    all_lane = np.arange(n * full)
    same_c = (k_row[:, None] == all_lane[None, :] // full) & (c_row[:, None] == all_lane[None, :] % full % CB)
    lane_v = np.where(all_lane % full < wide, all_lane % full // CB, -1).astype(np.int32)
    pick = jnp.where(jnp.asarray(same_c) & ((ka * local_v + jnp.asarray(v_row, jnp.int32))[:, None] == jnp.asarray(lane_v)[None, :]), 1.0, 0.0)
    pair_row = np.arange(pair_dev * band)
    same_row = band_row[:, None] % band == pair_row[None, :] % band
    slot_near = jnp.take(kpoint_slot, kpairs[:, 0])
    near_lane = jnp.repeat(slot_near, band)
    near = jnp.where(jnp.asarray(same_row) & (near_lane[None, :] == jnp.asarray(k_row, jnp.int32)[:, None]), 1.0, 0.0)
    smem = pl.BlockSpec(memory_space=pltpu.SMEM)
    result = pl.pallas_call(
        functools.partial(response_kernel, n, parts),
        out_shape=jax.ShapeDtypeStruct((trials, wide), jnp.float32),
        in_specs=[smem] * 2 + [vmem] * 6,
        out_specs=vmem,
        scratch_shapes=[
            pltpu.VMEM((VB, 2 * pair_dev, band, columns), jnp.bfloat16),
            pltpu.VMEM((2 * pair_dev * band, full), jnp.float32),
            pltpu.VMEM((2, pair_dev * band, n * full), jnp.bfloat16),
            pltpu.VMEM((every, n * full), jnp.bfloat16),
            pltpu.VMEM((every, n * full), jnp.bfloat16),
            pltpu.VMEM((n, parts, trials, full), jnp.float32),
            pltpu.VMEM((parts - 1, n, trials, full), jnp.float32),
            pltpu.VMEM((n, trials, full), jnp.float32),
            pltpu.VMEM((n - 1, trials, full), jnp.float32),
            dma((n, parts - 1)), dma((n, parts - 1)), dma((n - 1,)), dma((n - 1,)),
        ],
        compiler_params=pltpu.CompilerParams(collective_id=1, has_side_effects=True, vmem_limit_bytes=48 * 1024 * 1024),
    )(
        position, jnp.take(kpoint_slot, kpairs[:, 1]), kernel.reshape(slot_count, rows, columns), x_all,
        jnp.asarray(mask), jnp.asarray(spread), near.astype(jnp.bfloat16), pick.astype(jnp.bfloat16),
    )
    return result.reshape(1, trials * wide)


def slots(momentum, pair_dev, owners):
    capacity = max(2, 2 * pair_dev // owners)
    slot_count = owners * capacity
    target = momentum[:, 0]
    indices = jnp.arange(pair_dev, dtype=jnp.int32)
    earlier = (target[:, None] == target[None, :]) & (indices[None, :] < indices[:, None])
    position = target * capacity + jnp.sum(earlier.astype(jnp.int32), axis=1)
    matches = position[None, :] == jnp.arange(slot_count, dtype=jnp.int32)[:, None]
    source = jnp.sum(jnp.where(matches, indices[None, :], 0), axis=1)
    return capacity, slot_count, position, source


def local(valence, conduction, screened, momentum, kpairs, kpoint_slot, trial_blocks):
    n, parts = lax.axis_size("pb"), lax.axis_size("ka")
    if n >= 8 and n % 2 == 0 and parts == 4 and n * conduction.shape[2] * valence.shape[2] * 4 <= 16 * 1024 * 1024:
        return ringed(valence, conduction, screened, momentum, kpairs, kpoint_slot, trial_blocks)
    return routed(valence, conduction, screened, momentum, kpairs, kpoint_slot, trial_blocks)


def routed(valence, conduction, screened, momentum, kpairs, kpoint_slot, trial_blocks):
    highest = lax.Precision.HIGHEST
    pair_dev = valence.shape[0]
    owners = lax.axis_size("pb")
    capacity = max(2, 2 * pair_dev // owners)
    slot_count = owners * capacity
    target = momentum[:, 0]
    indices = jnp.arange(pair_dev, dtype=jnp.int32)
    earlier = (target[:, None] == target[None, :]) & (indices[None, :] < indices[:, None])
    position = target * capacity + jnp.sum(earlier.astype(jnp.int32), axis=1)
    matches = position[None, :] == jnp.arange(slot_count, dtype=jnp.int32)[:, None]
    source = jnp.sum(jnp.where(matches, indices[None, :], 0), axis=1)
    filled = jnp.any(matches, axis=1)
    outgoing = jnp.where(filled[:, None, None], jnp.take(valence, source, axis=0), 0.0)
    outgoing = outgoing.reshape(owners, capacity, valence.shape[1], valence.shape[2])
    matrix = screened[0]
    product = jnp.einsum(
        "scrg,gh->scrh",
        lax.all_to_all(outgoing, "pb", split_axis=0, concat_axis=0, tiled=True),
        matrix,
        precision=highest,
        preferred_element_type=jnp.float32,
    )
    returned = lax.all_to_all(product, "pb", split_axis=0, concat_axis=0, tiled=True)
    by_slot = returned.reshape(slot_count, returned.shape[2], returned.shape[3])
    rows_back = jnp.take(by_slot, position, axis=0)
    columns = lax.all_to_all(rows_back, "ka", split_axis=2, concat_axis=1, tiled=True)
    conduct_wide = conduction.astype(jnp.float32)
    partial_kernel = jnp.einsum(
        "prg,pbg->prb", columns, conduct_wide, precision=highest, preferred_element_type=jnp.float32
    )
    kernel = lax.psum(partial_kernel, "ka")
    gathered = lax.all_gather(trial_blocks, "pb", axis=0, tiled=True)
    kpoint_count = gathered.shape[0]
    local_trials = gathered.shape[1] // (VB * CB)
    blocks = gathered.reshape(kpoint_count, local_trials, VB, CB)
    slot_near = jnp.take(kpoint_slot, kpairs[:, 0])
    slot_far = jnp.take(kpoint_slot, kpairs[:, 1])
    near_trials = jnp.take(blocks, slot_near, axis=0)
    far_trials = jnp.take(blocks, slot_far, axis=0)
    kernel_blocks = kernel.reshape(pair_dev, VB, VB, CB, CB)
    direct = jnp.einsum("pvwcd,pnwd->pnvc", kernel_blocks, far_trials, precision=highest)
    mirror = jnp.einsum("pvwcd,pnvc->pnwd", kernel_blocks, near_trials, precision=highest)
    kpoint_rows = jnp.arange(kpoint_count, dtype=jnp.int32)[:, None]
    onehot_near = (slot_near[None, :] == kpoint_rows).astype(jnp.float32)
    onehot_far = (slot_far[None, :] == kpoint_rows).astype(jnp.float32)
    summed = jnp.dot(
        onehot_near,
        direct.reshape(pair_dev, -1),
        precision=highest,
        preferred_element_type=jnp.float32,
    )
    summed = summed + jnp.dot(
        onehot_far,
        mirror.reshape(pair_dev, -1),
        precision=highest,
        preferred_element_type=jnp.float32,
    )
    return lax.psum_scatter(summed, "pb", scatter_dimension=0, tiled=True)


def solution(mesh):
    return jax.shard_map(
        local,
        mesh=mesh,
        in_specs=(
            P("pb", "ka", None),
            P("pb", None, "ka"),
            P("pb", None, None),
            P("pb", None),
            P("pb", None),
            P(),
            P("pb", "ka"),
        ),
        out_specs=P("pb", "ka"),
        check_vma=False,
    )
```

```python
import functools

import jax
import jax.numpy as jnp
import numpy as np
from jax import lax
from jax.experimental import pallas as pl
from jax.experimental.pallas import tpu as pltpu
from jax.sharding import PartitionSpec as P

VB = 8
CB = 14
MESH = pl.DeviceIdType.MESH
NT = (((1,), (1,)), ((), ()))


def dot_nt(a, b):
    return lax.dot_general(a, b, NT, preferred_element_type=jnp.float32)


def halves(x):
    high = x.astype(jnp.bfloat16)
    return high, (x - high.astype(jnp.float32)).astype(jnp.bfloat16)


def ring_index(place, n):
    return jnp.where(place < n // 2, 2 * place, 2 * (n - 1 - place) + 1)


def kernel_blocks_kernel(
    n, parts, capacity,
    source_ref, v_ref, c_ref, w_ref, x_ref,
    k_ref, xout_ref,
    w_main, w_cross, v_all, v_high, v_low, stacked, b_high, b_low, k_part, k_near, k_go, k_got, x_all,
    local_sems, v_send, v_recv, ring_send, ring_recv, cross_send, cross_recv,
    near_send, near_recv, go_send, go_recv, x_send, x_recv, xk_send, xk_recv,
):
    pb, ka = lax.axis_index("pb"), lax.axis_index("ka")
    place = jnp.where(pb % 2 == 0, pb // 2, n - 1 - pb // 2)
    right = ring_index((place + 1) % n, n)
    left = ring_index((place + n - 1) % n, n)
    core = ka % 2
    partner = ka + 1 - 2 * core
    across = (ka + 2) % parts
    chip = ka - core
    other = (chip + 2) % parts
    rows = v_ref.shape[1]
    depth = w_main.shape[1]
    main = w_main.shape[2]
    half = depth // 2
    pairs = v_ref.shape[0]
    all_rows = parts * rows
    span = capacity * all_rows

    def at_block(index, count=1):
        return pl.ds(pl.multiple_of(index * depth, depth), count * depth)

    cross_rows = pl.ds(pl.multiple_of(core * half, half), half)
    loads = [
        pltpu.make_async_copy(w_ref.at[0, at_block(ka), at_block(ka)], w_main.at[place, :, pl.ds(0, depth)], local_sems.at[0]),
        pltpu.make_async_copy(
            w_ref.at[0, at_block(ka), at_block(other, 2)], w_main.at[place, :, pl.ds(depth, 2 * depth)], local_sems.at[1]
        ),
        pltpu.make_async_copy(
            w_ref.at[0, pl.ds(pl.multiple_of(chip * depth + core * half, half), half), at_block(chip + 1)],
            w_cross.at[place, cross_rows], local_sems.at[2],
        ),
        pltpu.make_async_copy(v_ref, v_all.at[ka], local_sems.at[3]),
    ]
    for load in loads:
        load.start()
    x_all[ka, pb] = x_ref[...]

    barrier = pltpu.get_barrier_semaphore()
    for d in range(1, n):
        pl.semaphore_signal(barrier, inc=1, device_id=((pb + d) % n, ka), device_id_type=MESH)
    for d in range(1, parts):
        pl.semaphore_signal(barrier, inc=1, device_id=(pb, (ka + d) % parts), device_id_type=MESH)
    pl.semaphore_wait(barrier, n + parts - 2)

    def remote(src, dst, send, recv, to):
        return pltpu.make_async_remote_copy(src_ref=src, dst_ref=dst, send_sem=send, recv_sem=recv, device_id=to, device_id_type=MESH)

    def ring(step):
        found = []
        for way, at, to in ((0, (place + n - step) % n, right), (1, (place + step) % n, left)):
            if step < n // 2 - 1:
                spans = (w_main.at[at], w_cross.at[at, cross_rows])
            else:
                quarter = half // 2
                spans = (
                    w_main.at[at, pl.ds(way * half, half)],
                    w_cross.at[at, pl.ds(pl.multiple_of(core * half + way * quarter, quarter), quarter)],
                )
            found.append([
                remote(part, part, ring_send.at[step, way, i], ring_recv.at[step, way, i], (to, ka)) for i, part in enumerate(spans)
            ])
        return found

    def cross_copy(at):
        part = w_cross.at[at, cross_rows]
        return remote(part, part, cross_send.at[at], cross_recv.at[at], (pb, partner))

    for load in loads:
        load.wait()
    v_across = remote(v_all.at[ka], v_all.at[ka], v_send.at[1], v_recv.at[1], (pb, across))
    v_partner = remote(v_all.at[ka], v_all.at[ka], v_send.at[0], v_recv.at[0], (pb, partner))
    v_pass = remote(v_all.at[across], v_all.at[across], v_send.at[2], v_recv.at[2], (pb, partner))
    copies = ring(0)
    for copy in copies[0] + copies[1]:
        copy.start()
    v_across.start()
    v_partner.start()
    cross_copy(place).start()
    x_copies = [
        remote(x_all.at[ka, pb], x_all.at[ka, pb], x_send.at[d - 1], x_recv.at[d - 1], ((pb + d) % n, ka)) for d in range(1, n)
    ]
    for copy in x_copies:
        copy.start()

    order = (ka, across, partner, (partner + 2) % parts)

    def split(p, carry):
        for i in range(parts):
            pieces = ((at_block(ka), 0, depth), (at_block(other, 2), depth, 2 * depth), (at_block(partner), main, depth))
            for columns, at, size in pieces:
                high, low = halves(v_all[order[i], p, :, columns])
                v_high[p, pl.ds(i * rows, rows), pl.ds(at, size)] = high
                v_low[p, pl.ds(i * rows, rows), pl.ds(at, size)] = low
        return carry

    def place_of(k):
        return (place + n + ((k + 1) // 2) * (2 * (k % 2) - 1)) % n

    def near_copy(q):
        return remote(k_part.at[q, :, pl.ds(2 * rows, 2 * rows), :], k_near.at[q], near_send.at[q], near_recv.at[q], (pb, partner))

    def go_copy(q):
        return remote(k_go.at[q], k_got.at[q], go_send.at[q], go_recv.at[q], (pb, across))

    def pass_on(k):
        q = ring_index(place_of(k), n)
        near_copy(q).wait()
        for s in range(capacity):
            k_go[q, s] = k_part[q, s, pl.ds(rows, rows), :] + k_near[q, s, pl.ds(rows, rows), :]
        go_copy(q).start()

    def block(k):
        at = place_of(k)
        q = ring_index(at, n)
        for s in range(capacity):
            p = source_ref[q * capacity + s]
            stacked[pl.ds(s * all_rows, all_rows), :] = v_high[p]
            stacked[pl.ds(span + s * all_rows, all_rows), :] = v_low[p]
        high, low = halves(w_main[at])
        b_high[:, pl.ds(0, main)] = high
        b_low[:, pl.ds(0, main)] = low
        cross_copy(at).wait()
        between = w_cross[at]
        high, low = halves(jnp.where(core == 0, between, between.T))
        b_high[:, pl.ds(main, depth)] = high
        b_low[:, pl.ds(main, depth)] = low
        both = dot_nt(stacked[...], b_high[...])
        screened = both[:span] + (both[span:] + dot_nt(stacked[pl.ds(0, span), :], b_low[...]))
        s_high, s_low = halves(screened)
        for s in range(capacity):
            part = slice(s * all_rows, (s + 1) * all_rows)
            conduct = c_ref[source_ref[q * capacity + s]]
            k_part[q, s] = dot_nt(s_high[part], conduct) + dot_nt(s_low[part], conduct)
        near_copy(q).start()

    def blocks(first, last):
        def one(k, carry):
            block(k)
            pass_on(k - 1)
            return carry

        lax.fori_loop(first, last, one, 0)

    for step in range(1, n // 2):
        later = ring(step)
        for way in range(2):
            for copy in copies[way]:
                copy.wait_recv()
            for copy in later[way]:
                copy.start()
            cross_copy(place_of(2 * step - way)).start()
        for copy in copies[0] + copies[1]:
            copy.wait_send()
        copies = later
        if step == 1:
            for copy in x_copies:
                copy.wait()
            xk_copies = [
                remote(x_all.at[ka], x_all.at[ka], xk_send.at[d - 1], xk_recv.at[d - 1], (pb, (ka + d) % parts))
                for d in range(1, parts)
            ]
            for copy in xk_copies:
                copy.start()
        if step == n // 2 - 2:
            v_across.wait()
            v_pass.start()
            v_partner.wait()
            v_pass.wait()
            lax.fori_loop(0, pairs, split, 0)
            block(0)
            blocks(1, n - 4)
        if step == n // 2 - 1:
            blocks(n - 4, n - 1)
            for copy in xk_copies:
                copy.wait()
            xout_ref[...] = x_all[...]
    for copy in copies[0] + copies[1]:
        copy.wait()
    cross_copy(place_of(n - 1)).start()
    blocks(n - 1, n)
    pass_on(n - 1)

    def total(q, carry):
        go_copy(q).wait()
        for s in range(capacity):
            k_ref[q, s] = (k_part[q, s, pl.ds(0, rows), :] + k_near[q, s, pl.ds(0, rows), :]) + k_got[q, s]
        return carry

    lax.fori_loop(0, n, total, 0)


def response_kernel(
    n, parts,
    position_ref, far_ref, k_ref, x_ref, mask_ref, spread_ref, near_ref, pick_ref,
    out_ref,
    wide_rows, mixed, by_far, x_high, x_low, given, landed, joined, landed_pb,
    ka_send, ka_recv, pb_send, pb_recv,
):
    pb, ka = lax.axis_index("pb"), lax.axis_index("ka")
    trials, wide = x_ref.shape[2:]
    full = spread_ref.shape[2]
    tall = mask_ref.shape[0]
    local_v = k_ref.shape[1] // VB
    band = local_v * tall
    pairs = position_ref.shape[0]
    barrier = pltpu.get_barrier_semaphore()
    for d in range(1, n):
        pl.semaphore_signal(barrier, inc=1, device_id=((pb + d) % n, ka), device_id_type=MESH)
    for d in range(1, parts):
        pl.semaphore_signal(barrier, inc=1, device_id=(pb, (ka + d) % parts), device_id_type=MESH)

    def dot(a, b):
        return jnp.dot(a, b, preferred_element_type=jnp.float32)

    x_high[...] = jnp.zeros_like(x_high)
    x_low[...] = jnp.zeros_like(x_low)
    for m in range(n):
        for j in range(parts):
            high, low = halves(x_ref[j, m])
            x_high[pl.ds(j * trials, trials), pl.ds(m * full, wide)] = high
            x_low[pl.ds(j * trials, trials), pl.ds(m * full, wide)] = low

    def fill(p, carry):
        values = k_ref[position_ref[p]]
        for w in range(VB):
            for v in range(local_v):
                row = values[v * VB + w:v * VB + w + 1]
                high, low = halves(jnp.broadcast_to(row, mask_ref.shape) * mask_ref[...])
                wide_rows[w, p, pl.ds(v * tall, tall), :] = high
                wide_rows[w, pairs + p, pl.ds(v * tall, tall), :] = low
        return carry

    lax.fori_loop(0, pairs, fill, 0)
    lanes = wide_rows.shape[-1]
    for w in range(VB):
        part = dot(wide_rows[w].reshape(2 * pairs * band, lanes), spread_ref[w])
        if w == 0:
            mixed[...] = part
        else:
            mixed[...] += part

    def cut(p, carry):
        at = pl.multiple_of(p * band, band)
        value = mixed[pl.ds(at, band), :] + mixed[pl.ds(pl.multiple_of((pairs + p) * band, band), band), :]
        for m in range(n):
            high, low = halves(value * (far_ref[p] == m).astype(jnp.float32))
            by_far[0, pl.ds(at, band), pl.ds(m * full, full)] = high
            by_far[1, pl.ds(at, band), pl.ds(m * full, full)] = low
        return carry

    lax.fori_loop(0, pairs, cut, 0)
    g_high, g_low = halves(dot(near_ref[...], by_far[0]) + dot(near_ref[...], by_far[1]))
    pick = pick_ref[...]
    p_high = dot_nt(x_high[...], pick).astype(jnp.bfloat16)
    p_low = dot_nt(x_low[...], pick).astype(jnp.bfloat16)
    direct = dot_nt(x_high[...], g_high) + (dot_nt(x_high[...], g_low) + dot_nt(x_low[...], g_high))
    d_high, d_low = halves(direct)
    value = dot(p_high, g_high) + (dot(p_high, g_low) + dot(p_low, g_high))
    value = value + (dot(d_high, pick) + dot(d_low, pick))
    for m in range(n):
        for j in range(parts):
            given[m, j] = value[j * trials:(j + 1) * trials, m * full:(m + 1) * full]
    pl.semaphore_wait(barrier, n + parts - 2)

    def remote(src, dst, send, recv, to):
        return pltpu.make_async_remote_copy(src_ref=src, dst_ref=dst, send_sem=send, recv_sem=recv, device_id=to, device_id_type=MESH)

    def ka_copy(m, d):
        to = (ka + d) % parts
        return remote(given.at[m, to], landed.at[d - 1, m], ka_send.at[m, d - 1], ka_recv.at[m, d - 1], (pb, to))

    def pb_copy(d):
        to = (pb + d) % n
        return remote(joined.at[to], landed_pb.at[d - 1], pb_send.at[d - 1], pb_recv.at[d - 1], (to, ka))

    def send(m, carry):
        for d in range(1, parts):
            ka_copy(m, d).start()
        return carry

    lax.fori_loop(0, n, send, 0)

    def join(m, carry):
        value = given[m, ka]
        for d in range(1, parts):
            ka_copy(m, d).wait()
            value = value + landed[d - 1, m]
        joined[m] = value
        return carry

    lax.fori_loop(0, n, join, 0)
    for d in range(1, n):
        pb_copy(d).start()
    value = joined[pb]
    for d in range(1, n):
        pb_copy(d).wait()
        value = value + landed_pb[d - 1]
    out_ref[...] = value[:, :wide]


def ringed(valence, conduction, screened, momentum, kpairs, kpoint_slot, trial_blocks):
    pair_dev, rows, waves = valence.shape
    n, parts = lax.axis_size("pb"), lax.axis_size("ka")
    capacity, slot_count, position, source = slots(momentum, pair_dev, n)
    trials = trial_blocks.shape[1] // (VB * CB)
    wide = VB * CB
    depth = conduction.shape[2]
    columns = conduction.shape[1]
    vmem = pl.BlockSpec(memory_space=pltpu.VMEM)
    any_space = pl.BlockSpec(memory_space=pl.ANY)
    dma = pltpu.SemaphoreType.DMA
    kernel, x_all = pl.pallas_call(
        functools.partial(kernel_blocks_kernel, n, parts, capacity),
        out_shape=(
            jax.ShapeDtypeStruct((n, capacity, rows, columns), jnp.float32),
            jax.ShapeDtypeStruct((parts, n, trials, wide), jnp.float32),
        ),
        in_specs=[pl.BlockSpec(memory_space=pltpu.SMEM), any_space, vmem, any_space, vmem],
        out_specs=(vmem, vmem),
        scratch_shapes=[
            pltpu.VMEM((n, depth, waves - depth), jnp.float32),
            pltpu.VMEM((n, depth, depth), jnp.float32),
            pltpu.VMEM((parts, pair_dev, rows, waves), jnp.float32),
            pltpu.VMEM((pair_dev, parts * rows, waves), jnp.bfloat16),
            pltpu.VMEM((pair_dev, parts * rows, waves), jnp.bfloat16),
            pltpu.VMEM((2 * capacity * parts * rows, waves), jnp.bfloat16),
            pltpu.VMEM((depth, waves), jnp.bfloat16),
            pltpu.VMEM((depth, waves), jnp.bfloat16),
            pltpu.VMEM((n, capacity, parts * rows, columns), jnp.float32),
            pltpu.VMEM((n, capacity, 2 * rows, columns), jnp.float32),
            pltpu.VMEM((n, capacity, rows, columns), jnp.float32),
            pltpu.VMEM((n, capacity, rows, columns), jnp.float32),
            pltpu.VMEM((parts, n, trials, wide), jnp.float32),
            dma((4,)), dma((3,)), dma((3,)), dma((n // 2, 2, 2)), dma((n // 2, 2, 2)), dma((n,)), dma((n,)),
            dma((n,)), dma((n,)), dma((n,)), dma((n,)), dma((n - 1,)), dma((n - 1,)), dma((parts - 1,)), dma((parts - 1,)),
        ],
        compiler_params=pltpu.CompilerParams(collective_id=0, has_side_effects=True, vmem_limit_bytes=56 * 1024 * 1024),
    )(source, valence, conduction, screened, trial_blocks.reshape(trials, wide))
    ka = lax.axis_index("ka")
    local_v = rows // VB
    tall = -(-CB // 16) * 16
    band = local_v * tall
    every = parts * trials
    full = -(-wide // 128) * 128
    c_of, d_of = np.arange(columns) // CB, np.arange(columns) % CB
    lane = np.arange(full)
    w_to, d_to = lane // CB, lane % CB
    mask = (np.arange(tall)[:, None] == c_of[None, :]).astype(np.float32)
    at_w = (w_to[None, None, :] == np.arange(VB)[:, None, None]) & (lane < wide)[None, None, :]
    spread = ((d_of[:, None] == d_to[None, :])[None] & at_w).astype(jnp.bfloat16)
    band_row = np.arange(n * band)
    k_row, v_row, c_row = band_row // band, band_row % band // tall, band_row % tall
    all_lane = np.arange(n * full)
    same_c = (k_row[:, None] == all_lane[None, :] // full) & (c_row[:, None] == all_lane[None, :] % full % CB)
    lane_v = np.where(all_lane % full < wide, all_lane % full // CB, -1).astype(np.int32)
    pick = jnp.where(jnp.asarray(same_c) & ((ka * local_v + jnp.asarray(v_row, jnp.int32))[:, None] == jnp.asarray(lane_v)[None, :]), 1.0, 0.0)
    pair_row = np.arange(pair_dev * band)
    same_row = band_row[:, None] % band == pair_row[None, :] % band
    slot_near = jnp.take(kpoint_slot, kpairs[:, 0])
    near_lane = jnp.repeat(slot_near, band)
    near = jnp.where(jnp.asarray(same_row) & (near_lane[None, :] == jnp.asarray(k_row, jnp.int32)[:, None]), 1.0, 0.0)
    smem = pl.BlockSpec(memory_space=pltpu.SMEM)
    result = pl.pallas_call(
        functools.partial(response_kernel, n, parts),
        out_shape=jax.ShapeDtypeStruct((trials, wide), jnp.float32),
        in_specs=[smem] * 2 + [vmem] * 6,
        out_specs=vmem,
        scratch_shapes=[
            pltpu.VMEM((VB, 2 * pair_dev, band, columns), jnp.bfloat16),
            pltpu.VMEM((2 * pair_dev * band, full), jnp.float32),
            pltpu.VMEM((2, pair_dev * band, n * full), jnp.bfloat16),
            pltpu.VMEM((every, n * full), jnp.bfloat16),
            pltpu.VMEM((every, n * full), jnp.bfloat16),
            pltpu.VMEM((n, parts, trials, full), jnp.float32),
            pltpu.VMEM((parts - 1, n, trials, full), jnp.float32),
            pltpu.VMEM((n, trials, full), jnp.float32),
            pltpu.VMEM((n - 1, trials, full), jnp.float32),
            dma((n, parts - 1)), dma((n, parts - 1)), dma((n - 1,)), dma((n - 1,)),
        ],
        compiler_params=pltpu.CompilerParams(collective_id=1, has_side_effects=True, vmem_limit_bytes=48 * 1024 * 1024),
    )(
        position, jnp.take(kpoint_slot, kpairs[:, 1]), kernel.reshape(slot_count, rows, columns), x_all,
        jnp.asarray(mask), jnp.asarray(spread), near.astype(jnp.bfloat16), pick.astype(jnp.bfloat16),
    )
    return result.reshape(1, trials * wide)


def slots(momentum, pair_dev, owners):
    capacity = max(2, 2 * pair_dev // owners)
    slot_count = owners * capacity
    target = momentum[:, 0]
    indices = jnp.arange(pair_dev, dtype=jnp.int32)
    earlier = (target[:, None] == target[None, :]) & (indices[None, :] < indices[:, None])
    position = target * capacity + jnp.sum(earlier.astype(jnp.int32), axis=1)
    matches = position[None, :] == jnp.arange(slot_count, dtype=jnp.int32)[:, None]
    source = jnp.sum(jnp.where(matches, indices[None, :], 0), axis=1)
    return capacity, slot_count, position, source


def local(valence, conduction, screened, momentum, kpairs, kpoint_slot, trial_blocks):
    n, parts = lax.axis_size("pb"), lax.axis_size("ka")
    if n >= 8 and n % 2 == 0 and parts == 4 and n * conduction.shape[2] * valence.shape[2] * 4 <= 16 * 1024 * 1024:
        return ringed(valence, conduction, screened, momentum, kpairs, kpoint_slot, trial_blocks)
    return routed(valence, conduction, screened, momentum, kpairs, kpoint_slot, trial_blocks)


def routed(valence, conduction, screened, momentum, kpairs, kpoint_slot, trial_blocks):
    highest = lax.Precision.HIGHEST
    pair_dev = valence.shape[0]
    owners = lax.axis_size("pb")
    capacity = max(2, 2 * pair_dev // owners)
    slot_count = owners * capacity
    target = momentum[:, 0]
    indices = jnp.arange(pair_dev, dtype=jnp.int32)
    earlier = (target[:, None] == target[None, :]) & (indices[None, :] < indices[:, None])
    position = target * capacity + jnp.sum(earlier.astype(jnp.int32), axis=1)
    matches = position[None, :] == jnp.arange(slot_count, dtype=jnp.int32)[:, None]
    source = jnp.sum(jnp.where(matches, indices[None, :], 0), axis=1)
    filled = jnp.any(matches, axis=1)
    outgoing = jnp.where(filled[:, None, None], jnp.take(valence, source, axis=0), 0.0)
    outgoing = outgoing.reshape(owners, capacity, valence.shape[1], valence.shape[2])
    matrix = screened[0]
    product = jnp.einsum(
        "scrg,gh->scrh",
        lax.all_to_all(outgoing, "pb", split_axis=0, concat_axis=0, tiled=True),
        matrix,
        precision=highest,
        preferred_element_type=jnp.float32,
    )
    returned = lax.all_to_all(product, "pb", split_axis=0, concat_axis=0, tiled=True)
    by_slot = returned.reshape(slot_count, returned.shape[2], returned.shape[3])
    rows_back = jnp.take(by_slot, position, axis=0)
    columns = lax.all_to_all(rows_back, "ka", split_axis=2, concat_axis=1, tiled=True)
    conduct_wide = conduction.astype(jnp.float32)
    partial_kernel = jnp.einsum(
        "prg,pbg->prb", columns, conduct_wide, precision=highest, preferred_element_type=jnp.float32
    )
    kernel = lax.psum(partial_kernel, "ka")
    gathered = lax.all_gather(trial_blocks, "pb", axis=0, tiled=True)
    kpoint_count = gathered.shape[0]
    local_trials = gathered.shape[1] // (VB * CB)
    blocks = gathered.reshape(kpoint_count, local_trials, VB, CB)
    slot_near = jnp.take(kpoint_slot, kpairs[:, 0])
    slot_far = jnp.take(kpoint_slot, kpairs[:, 1])
    near_trials = jnp.take(blocks, slot_near, axis=0)
    far_trials = jnp.take(blocks, slot_far, axis=0)
    kernel_blocks = kernel.reshape(pair_dev, VB, VB, CB, CB)
    direct = jnp.einsum("pvwcd,pnwd->pnvc", kernel_blocks, far_trials, precision=highest)
    mirror = jnp.einsum("pvwcd,pnvc->pnwd", kernel_blocks, near_trials, precision=highest)
    kpoint_rows = jnp.arange(kpoint_count, dtype=jnp.int32)[:, None]
    onehot_near = (slot_near[None, :] == kpoint_rows).astype(jnp.float32)
    onehot_far = (slot_far[None, :] == kpoint_rows).astype(jnp.float32)
    summed = jnp.dot(
        onehot_near,
        direct.reshape(pair_dev, -1),
        precision=highest,
        preferred_element_type=jnp.float32,
    )
    summed = summed + jnp.dot(
        onehot_far,
        mirror.reshape(pair_dev, -1),
        precision=highest,
        preferred_element_type=jnp.float32,
    )
    return lax.psum_scatter(summed, "pb", scatter_dimension=0, tiled=True)


def solution(mesh):
    return jax.shard_map(
        local,
        mesh=mesh,
        in_specs=(
            P("pb", "ka", None),
            P("pb", None, "ka"),
            P("pb", None, None),
            P("pb", None),
            P("pb", None),
            P(),
            P("pb", "ka"),
        ),
        out_specs=P("pb", "ka"),
        check_vma=False,
    )
```

```python
import functools

import jax
import jax.numpy as jnp
import numpy as np
from jax import lax
from jax.experimental import pallas as pl
from jax.experimental.pallas import tpu as pltpu
from jax.sharding import PartitionSpec as P

VB = 8
CB = 14
MESH = pl.DeviceIdType.MESH
NT = (((1,), (1,)), ((), ()))


def dot_nt(a, b):
    return lax.dot_general(a, b, NT, preferred_element_type=jnp.float32)


def halves(x):
    high = x.astype(jnp.bfloat16)
    return high, (x - high.astype(jnp.float32)).astype(jnp.bfloat16)


def ring_index(place, n):
    return jnp.where(place < n // 2, 2 * place, 2 * (n - 1 - place) + 1)


def kernel_blocks_kernel(
    n, parts, capacity,
    source_ref, v_ref, c_ref, w_ref, x_ref,
    k_ref, xout_ref,
    w_main, w_cross, v_all, v_high, v_low, stacked, b_high, b_low, k_part, k_near, k_go, k_got, x_all,
    local_sems, v_send, v_recv, ring_send, ring_recv, cross_send, cross_recv,
    near_send, near_recv, go_send, go_recv, x_send, x_recv, xk_send, xk_recv,
):
    pb, ka = lax.axis_index("pb"), lax.axis_index("ka")
    place = jnp.where(pb % 2 == 0, pb // 2, n - 1 - pb // 2)
    right = ring_index((place + 1) % n, n)
    left = ring_index((place + n - 1) % n, n)
    core = ka % 2
    partner = ka + 1 - 2 * core
    across = (ka + 2) % parts
    chip = ka - core
    other = (chip + 2) % parts
    rows = v_ref.shape[1]
    depth = w_main.shape[1]
    main = w_main.shape[2]
    half = depth // 2
    pairs = v_ref.shape[0]
    all_rows = parts * rows
    span = capacity * all_rows

    def at_block(index, count=1):
        return pl.ds(pl.multiple_of(index * depth, depth), count * depth)

    cross_rows = pl.ds(pl.multiple_of(core * half, half), half)
    loads = [
        pltpu.make_async_copy(w_ref.at[0, at_block(ka), at_block(ka)], w_main.at[place, :, pl.ds(0, depth)], local_sems.at[0]),
        pltpu.make_async_copy(
            w_ref.at[0, at_block(ka), at_block(other, 2)], w_main.at[place, :, pl.ds(depth, 2 * depth)], local_sems.at[1]
        ),
        pltpu.make_async_copy(
            w_ref.at[0, pl.ds(pl.multiple_of(chip * depth + core * half, half), half), at_block(chip + 1)],
            w_cross.at[place, cross_rows], local_sems.at[2],
        ),
        pltpu.make_async_copy(v_ref, v_all.at[ka], local_sems.at[3]),
    ]
    for load in loads:
        load.start()
    x_all[ka, pb] = x_ref[...]

    barrier = pltpu.get_barrier_semaphore()
    for d in range(1, n):
        pl.semaphore_signal(barrier, inc=1, device_id=((pb + d) % n, ka), device_id_type=MESH)
    for d in range(1, parts):
        pl.semaphore_signal(barrier, inc=1, device_id=(pb, (ka + d) % parts), device_id_type=MESH)
    pl.semaphore_wait(barrier, n + parts - 2)

    def remote(src, dst, send, recv, to):
        return pltpu.make_async_remote_copy(src_ref=src, dst_ref=dst, send_sem=send, recv_sem=recv, device_id=to, device_id_type=MESH)

    def ring(step):
        found = []
        for way, at, to in ((0, (place + n - step) % n, right), (1, (place + step) % n, left)):
            if step < n // 2 - 1:
                spans = (w_main.at[at], w_cross.at[at, cross_rows])
            else:
                quarter = half // 2
                spans = (
                    w_main.at[at, pl.ds(way * half, half)],
                    w_cross.at[at, pl.ds(pl.multiple_of(core * half + way * quarter, quarter), quarter)],
                )
            found.append([
                remote(part, part, ring_send.at[step, way, i], ring_recv.at[step, way, i], (to, ka)) for i, part in enumerate(spans)
            ])
        return found

    def cross_copy(at):
        part = w_cross.at[at, cross_rows]
        return remote(part, part, cross_send.at[at], cross_recv.at[at], (pb, partner))

    for load in loads:
        load.wait()
    v_across = remote(v_all.at[ka], v_all.at[ka], v_send.at[1], v_recv.at[1], (pb, across))
    v_partner = remote(v_all.at[ka], v_all.at[ka], v_send.at[0], v_recv.at[0], (pb, partner))
    v_pass = remote(v_all.at[across], v_all.at[across], v_send.at[2], v_recv.at[2], (pb, partner))
    copies = ring(0)
    for copy in copies[0] + copies[1]:
        copy.start()
    v_across.start()
    v_partner.start()
    cross_copy(place).start()
    x_copies = [
        remote(x_all.at[ka, pb], x_all.at[ka, pb], x_send.at[d - 1], x_recv.at[d - 1], ((pb + d) % n, ka)) for d in range(1, n)
    ]
    for copy in x_copies:
        copy.start()

    order = (ka, across, partner, (partner + 2) % parts)

    def split(kinds, p, carry):
        for i in kinds:
            pieces = ((at_block(ka), 0, depth), (at_block(other, 2), depth, 2 * depth), (at_block(partner), main, depth))
            for columns, at, size in pieces:
                high, low = halves(v_all[order[i], p, :, columns])
                v_high[p, pl.ds(i * rows, rows), pl.ds(at, size)] = high
                v_low[p, pl.ds(i * rows, rows), pl.ds(at, size)] = low
        return carry

    def place_of(k):
        return (place + n + ((k + 1) // 2) * (2 * (k % 2) - 1)) % n

    def near_copy(q):
        return remote(k_part.at[q, :, pl.ds(2 * rows, 2 * rows), :], k_near.at[q], near_send.at[q], near_recv.at[q], (pb, partner))

    def go_copy(q):
        return remote(k_go.at[q], k_got.at[q], go_send.at[q], go_recv.at[q], (pb, across))

    def pass_on(k):
        q = ring_index(place_of(k), n)
        near_copy(q).wait()
        for s in range(capacity):
            k_go[q, s] = k_part[q, s, pl.ds(rows, rows), :] + k_near[q, s, pl.ds(rows, rows), :]
        go_copy(q).start()

    def block(k):
        at = place_of(k)
        q = ring_index(at, n)
        for s in range(capacity):
            p = source_ref[q * capacity + s]
            stacked[pl.ds(s * all_rows, all_rows), :] = v_high[p]
            stacked[pl.ds(span + s * all_rows, all_rows), :] = v_low[p]
        high, low = halves(w_main[at])
        b_high[:, pl.ds(0, main)] = high
        b_low[:, pl.ds(0, main)] = low
        cross_copy(at).wait()
        between = w_cross[at]
        high, low = halves(jnp.where(core == 0, between, between.T))
        b_high[:, pl.ds(main, depth)] = high
        b_low[:, pl.ds(main, depth)] = low
        both = dot_nt(stacked[...], b_high[...])
        screened = both[:span] + (both[span:] + dot_nt(stacked[pl.ds(0, span), :], b_low[...]))
        s_high, s_low = halves(screened)
        for s in range(capacity):
            part = slice(s * all_rows, (s + 1) * all_rows)
            conduct = c_ref[source_ref[q * capacity + s]]
            k_part[q, s] = dot_nt(s_high[part], conduct) + dot_nt(s_low[part], conduct)
        near_copy(q).start()

    def blocks(first, last):
        def one(k, carry):
            block(k)
            pass_on(k - 1)
            return carry

        lax.fori_loop(first, last, one, 0)

    v_partner.wait()
    lax.fori_loop(0, pairs, functools.partial(split, (0, 2)), 0)
    for step in range(1, n // 2):
        later = ring(step)
        for way in range(2):
            for landed, follow in zip(copies[way], later[way]):
                landed.wait_recv()
                follow.start()
            cross_copy(place_of(2 * step - way)).start()
        for copy in copies[0] + copies[1]:
            copy.wait_send()
        copies = later
        if step == 1:
            for copy in x_copies:
                copy.wait()
            xk_copies = [
                remote(x_all.at[ka], x_all.at[ka], xk_send.at[d - 1], xk_recv.at[d - 1], (pb, (ka + d) % parts))
                for d in range(1, parts)
            ]
            for copy in xk_copies:
                copy.start()
        if step == n // 2 - 2:
            v_across.wait()
            v_pass.start()
            v_pass.wait()
            lax.fori_loop(0, pairs, functools.partial(split, (1, 3)), 0)
            block(0)
            blocks(1, n - 5)
            for copy in xk_copies:
                copy.wait()
            xout_ref[...] = x_all[...]
        if step == n // 2 - 1:
            blocks(n - 5, n - 1)
    for copy in copies[0] + copies[1]:
        copy.wait()
    cross_copy(place_of(n - 1)).start()
    blocks(n - 1, n)
    pass_on(n - 1)

    def total(q, carry):
        go_copy(q).wait()
        for s in range(capacity):
            k_ref[q, s] = (k_part[q, s, pl.ds(0, rows), :] + k_near[q, s, pl.ds(0, rows), :]) + k_got[q, s]
        return carry

    lax.fori_loop(0, n, total, 0)


def response_kernel(
    n, parts,
    position_ref, far_ref, k_ref, x_ref, mask_ref, spread_ref, near_ref, pick_ref,
    out_ref,
    wide_rows, mixed, by_far, x_high, x_low, given, landed, joined, landed_pb,
    ka_send, ka_recv, pb_send, pb_recv,
):
    pb, ka = lax.axis_index("pb"), lax.axis_index("ka")
    trials, wide = x_ref.shape[2:]
    full = spread_ref.shape[2]
    tall = mask_ref.shape[0]
    local_v = k_ref.shape[1] // VB
    band = local_v * tall
    pairs = position_ref.shape[0]
    barrier = pltpu.get_barrier_semaphore()
    for d in range(1, n):
        pl.semaphore_signal(barrier, inc=1, device_id=((pb + d) % n, ka), device_id_type=MESH)
    for d in range(1, parts):
        pl.semaphore_signal(barrier, inc=1, device_id=(pb, (ka + d) % parts), device_id_type=MESH)

    def dot(a, b):
        return jnp.dot(a, b, preferred_element_type=jnp.float32)

    x_high[...] = jnp.zeros_like(x_high)
    x_low[...] = jnp.zeros_like(x_low)
    for m in range(n):
        for j in range(parts):
            high, low = halves(x_ref[j, m])
            x_high[pl.ds(j * trials, trials), pl.ds(m * full, wide)] = high
            x_low[pl.ds(j * trials, trials), pl.ds(m * full, wide)] = low

    def fill(p, carry):
        values = k_ref[position_ref[p]]
        for w in range(VB):
            for v in range(local_v):
                row = values[v * VB + w:v * VB + w + 1]
                high, low = halves(jnp.broadcast_to(row, mask_ref.shape) * mask_ref[...])
                wide_rows[w, p, pl.ds(v * tall, tall), :] = high
                wide_rows[w, pairs + p, pl.ds(v * tall, tall), :] = low
        return carry

    lax.fori_loop(0, pairs, fill, 0)
    lanes = wide_rows.shape[-1]
    for w in range(VB):
        part = dot(wide_rows[w].reshape(2 * pairs * band, lanes), spread_ref[w])
        if w == 0:
            mixed[...] = part
        else:
            mixed[...] += part

    def cut(p, carry):
        at = pl.multiple_of(p * band, band)
        value = mixed[pl.ds(at, band), :] + mixed[pl.ds(pl.multiple_of((pairs + p) * band, band), band), :]
        for m in range(n):
            high, low = halves(value * (far_ref[p] == m).astype(jnp.float32))
            by_far[0, pl.ds(at, band), pl.ds(m * full, full)] = high
            by_far[1, pl.ds(at, band), pl.ds(m * full, full)] = low
        return carry

    lax.fori_loop(0, pairs, cut, 0)
    g_high, g_low = halves(dot(near_ref[...], by_far[0]) + dot(near_ref[...], by_far[1]))
    pick = pick_ref[...]
    p_high = dot_nt(x_high[...], pick).astype(jnp.bfloat16)
    p_low = dot_nt(x_low[...], pick).astype(jnp.bfloat16)
    direct = dot_nt(x_high[...], g_high) + (dot_nt(x_high[...], g_low) + dot_nt(x_low[...], g_high))
    d_high, d_low = halves(direct)
    value = dot(p_high, g_high) + (dot(p_high, g_low) + dot(p_low, g_high))
    value = value + (dot(d_high, pick) + dot(d_low, pick))
    for m in range(n):
        for j in range(parts):
            given[m, j] = value[j * trials:(j + 1) * trials, m * full:(m + 1) * full]
    pl.semaphore_wait(barrier, n + parts - 2)

    def remote(src, dst, send, recv, to):
        return pltpu.make_async_remote_copy(src_ref=src, dst_ref=dst, send_sem=send, recv_sem=recv, device_id=to, device_id_type=MESH)

    def ka_copy(m, d):
        to = (ka + d) % parts
        return remote(given.at[m, to], landed.at[d - 1, m], ka_send.at[m, d - 1], ka_recv.at[m, d - 1], (pb, to))

    def pb_copy(d):
        to = (pb + d) % n
        return remote(joined.at[to], landed_pb.at[d - 1], pb_send.at[d - 1], pb_recv.at[d - 1], (to, ka))

    def send(m, carry):
        for d in range(1, parts):
            ka_copy(m, d).start()
        return carry

    lax.fori_loop(0, n, send, 0)

    def join(m, carry):
        value = given[m, ka]
        for d in range(1, parts):
            ka_copy(m, d).wait()
            value = value + landed[d - 1, m]
        joined[m] = value
        return carry

    lax.fori_loop(0, n, join, 0)
    for d in range(1, n):
        pb_copy(d).start()
    value = joined[pb]
    for d in range(1, n):
        pb_copy(d).wait()
        value = value + landed_pb[d - 1]
    out_ref[...] = value[:, :wide]


def ringed(valence, conduction, screened, momentum, kpairs, kpoint_slot, trial_blocks):
    pair_dev, rows, waves = valence.shape
    n, parts = lax.axis_size("pb"), lax.axis_size("ka")
    capacity, slot_count, position, source = slots(momentum, pair_dev, n)
    trials = trial_blocks.shape[1] // (VB * CB)
    wide = VB * CB
    depth = conduction.shape[2]
    columns = conduction.shape[1]
    vmem = pl.BlockSpec(memory_space=pltpu.VMEM)
    any_space = pl.BlockSpec(memory_space=pl.ANY)
    dma = pltpu.SemaphoreType.DMA
    kernel, x_all = pl.pallas_call(
        functools.partial(kernel_blocks_kernel, n, parts, capacity),
        out_shape=(
            jax.ShapeDtypeStruct((n, capacity, rows, columns), jnp.float32),
            jax.ShapeDtypeStruct((parts, n, trials, wide), jnp.float32),
        ),
        in_specs=[pl.BlockSpec(memory_space=pltpu.SMEM), any_space, vmem, any_space, vmem],
        out_specs=(vmem, vmem),
        scratch_shapes=[
            pltpu.VMEM((n, depth, waves - depth), jnp.float32),
            pltpu.VMEM((n, depth, depth), jnp.float32),
            pltpu.VMEM((parts, pair_dev, rows, waves), jnp.float32),
            pltpu.VMEM((pair_dev, parts * rows, waves), jnp.bfloat16),
            pltpu.VMEM((pair_dev, parts * rows, waves), jnp.bfloat16),
            pltpu.VMEM((2 * capacity * parts * rows, waves), jnp.bfloat16),
            pltpu.VMEM((depth, waves), jnp.bfloat16),
            pltpu.VMEM((depth, waves), jnp.bfloat16),
            pltpu.VMEM((n, capacity, parts * rows, columns), jnp.float32),
            pltpu.VMEM((n, capacity, 2 * rows, columns), jnp.float32),
            pltpu.VMEM((n, capacity, rows, columns), jnp.float32),
            pltpu.VMEM((n, capacity, rows, columns), jnp.float32),
            pltpu.VMEM((parts, n, trials, wide), jnp.float32),
            dma((4,)), dma((3,)), dma((3,)), dma((n // 2, 2, 2)), dma((n // 2, 2, 2)), dma((n,)), dma((n,)),
            dma((n,)), dma((n,)), dma((n,)), dma((n,)), dma((n - 1,)), dma((n - 1,)), dma((parts - 1,)), dma((parts - 1,)),
        ],
        compiler_params=pltpu.CompilerParams(collective_id=0, has_side_effects=True, vmem_limit_bytes=56 * 1024 * 1024),
    )(source, valence, conduction, screened, trial_blocks.reshape(trials, wide))
    ka = lax.axis_index("ka")
    local_v = rows // VB
    tall = -(-CB // 16) * 16
    band = local_v * tall
    every = parts * trials
    full = -(-wide // 128) * 128
    c_of, d_of = np.arange(columns) // CB, np.arange(columns) % CB
    lane = np.arange(full)
    w_to, d_to = lane // CB, lane % CB
    mask = (np.arange(tall)[:, None] == c_of[None, :]).astype(np.float32)
    at_w = (w_to[None, None, :] == np.arange(VB)[:, None, None]) & (lane < wide)[None, None, :]
    spread = ((d_of[:, None] == d_to[None, :])[None] & at_w).astype(jnp.bfloat16)
    band_row = np.arange(n * band)
    k_row, v_row, c_row = band_row // band, band_row % band // tall, band_row % tall
    all_lane = np.arange(n * full)
    same_c = (k_row[:, None] == all_lane[None, :] // full) & (c_row[:, None] == all_lane[None, :] % full % CB)
    lane_v = np.where(all_lane % full < wide, all_lane % full // CB, -1).astype(np.int32)
    pick = jnp.where(jnp.asarray(same_c) & ((ka * local_v + jnp.asarray(v_row, jnp.int32))[:, None] == jnp.asarray(lane_v)[None, :]), 1.0, 0.0)
    pair_row = np.arange(pair_dev * band)
    same_row = band_row[:, None] % band == pair_row[None, :] % band
    slot_near = jnp.take(kpoint_slot, kpairs[:, 0])
    near_lane = jnp.repeat(slot_near, band)
    near = jnp.where(jnp.asarray(same_row) & (near_lane[None, :] == jnp.asarray(k_row, jnp.int32)[:, None]), 1.0, 0.0)
    smem = pl.BlockSpec(memory_space=pltpu.SMEM)
    result = pl.pallas_call(
        functools.partial(response_kernel, n, parts),
        out_shape=jax.ShapeDtypeStruct((trials, wide), jnp.float32),
        in_specs=[smem] * 2 + [vmem] * 6,
        out_specs=vmem,
        scratch_shapes=[
            pltpu.VMEM((VB, 2 * pair_dev, band, columns), jnp.bfloat16),
            pltpu.VMEM((2 * pair_dev * band, full), jnp.float32),
            pltpu.VMEM((2, pair_dev * band, n * full), jnp.bfloat16),
            pltpu.VMEM((every, n * full), jnp.bfloat16),
            pltpu.VMEM((every, n * full), jnp.bfloat16),
            pltpu.VMEM((n, parts, trials, full), jnp.float32),
            pltpu.VMEM((parts - 1, n, trials, full), jnp.float32),
            pltpu.VMEM((n, trials, full), jnp.float32),
            pltpu.VMEM((n - 1, trials, full), jnp.float32),
            dma((n, parts - 1)), dma((n, parts - 1)), dma((n - 1,)), dma((n - 1,)),
        ],
        compiler_params=pltpu.CompilerParams(collective_id=1, has_side_effects=True, vmem_limit_bytes=48 * 1024 * 1024),
    )(
        position, jnp.take(kpoint_slot, kpairs[:, 1]), kernel.reshape(slot_count, rows, columns), x_all,
        jnp.asarray(mask), jnp.asarray(spread), near.astype(jnp.bfloat16), pick.astype(jnp.bfloat16),
    )
    return result.reshape(1, trials * wide)


def slots(momentum, pair_dev, owners):
    capacity = max(2, 2 * pair_dev // owners)
    slot_count = owners * capacity
    target = momentum[:, 0]
    indices = jnp.arange(pair_dev, dtype=jnp.int32)
    earlier = (target[:, None] == target[None, :]) & (indices[None, :] < indices[:, None])
    position = target * capacity + jnp.sum(earlier.astype(jnp.int32), axis=1)
    matches = position[None, :] == jnp.arange(slot_count, dtype=jnp.int32)[:, None]
    source = jnp.sum(jnp.where(matches, indices[None, :], 0), axis=1)
    return capacity, slot_count, position, source


def local(valence, conduction, screened, momentum, kpairs, kpoint_slot, trial_blocks):
    n, parts = lax.axis_size("pb"), lax.axis_size("ka")
    if n >= 8 and n % 2 == 0 and parts == 4 and n * conduction.shape[2] * valence.shape[2] * 4 <= 16 * 1024 * 1024:
        return ringed(valence, conduction, screened, momentum, kpairs, kpoint_slot, trial_blocks)
    return routed(valence, conduction, screened, momentum, kpairs, kpoint_slot, trial_blocks)


def routed(valence, conduction, screened, momentum, kpairs, kpoint_slot, trial_blocks):
    highest = lax.Precision.HIGHEST
    pair_dev = valence.shape[0]
    owners = lax.axis_size("pb")
    capacity = max(2, 2 * pair_dev // owners)
    slot_count = owners * capacity
    target = momentum[:, 0]
    indices = jnp.arange(pair_dev, dtype=jnp.int32)
    earlier = (target[:, None] == target[None, :]) & (indices[None, :] < indices[:, None])
    position = target * capacity + jnp.sum(earlier.astype(jnp.int32), axis=1)
    matches = position[None, :] == jnp.arange(slot_count, dtype=jnp.int32)[:, None]
    source = jnp.sum(jnp.where(matches, indices[None, :], 0), axis=1)
    filled = jnp.any(matches, axis=1)
    outgoing = jnp.where(filled[:, None, None], jnp.take(valence, source, axis=0), 0.0)
    outgoing = outgoing.reshape(owners, capacity, valence.shape[1], valence.shape[2])
    matrix = screened[0]
    product = jnp.einsum(
        "scrg,gh->scrh",
        lax.all_to_all(outgoing, "pb", split_axis=0, concat_axis=0, tiled=True),
        matrix,
        precision=highest,
        preferred_element_type=jnp.float32,
    )
    returned = lax.all_to_all(product, "pb", split_axis=0, concat_axis=0, tiled=True)
    by_slot = returned.reshape(slot_count, returned.shape[2], returned.shape[3])
    rows_back = jnp.take(by_slot, position, axis=0)
    columns = lax.all_to_all(rows_back, "ka", split_axis=2, concat_axis=1, tiled=True)
    conduct_wide = conduction.astype(jnp.float32)
    partial_kernel = jnp.einsum(
        "prg,pbg->prb", columns, conduct_wide, precision=highest, preferred_element_type=jnp.float32
    )
    kernel = lax.psum(partial_kernel, "ka")
    gathered = lax.all_gather(trial_blocks, "pb", axis=0, tiled=True)
    kpoint_count = gathered.shape[0]
    local_trials = gathered.shape[1] // (VB * CB)
    blocks = gathered.reshape(kpoint_count, local_trials, VB, CB)
    slot_near = jnp.take(kpoint_slot, kpairs[:, 0])
    slot_far = jnp.take(kpoint_slot, kpairs[:, 1])
    near_trials = jnp.take(blocks, slot_near, axis=0)
    far_trials = jnp.take(blocks, slot_far, axis=0)
    kernel_blocks = kernel.reshape(pair_dev, VB, VB, CB, CB)
    direct = jnp.einsum("pvwcd,pnwd->pnvc", kernel_blocks, far_trials, precision=highest)
    mirror = jnp.einsum("pvwcd,pnvc->pnwd", kernel_blocks, near_trials, precision=highest)
    kpoint_rows = jnp.arange(kpoint_count, dtype=jnp.int32)[:, None]
    onehot_near = (slot_near[None, :] == kpoint_rows).astype(jnp.float32)
    onehot_far = (slot_far[None, :] == kpoint_rows).astype(jnp.float32)
    summed = jnp.dot(
        onehot_near,
        direct.reshape(pair_dev, -1),
        precision=highest,
        preferred_element_type=jnp.float32,
    )
    summed = summed + jnp.dot(
        onehot_far,
        mirror.reshape(pair_dev, -1),
        precision=highest,
        preferred_element_type=jnp.float32,
    )
    return lax.psum_scatter(summed, "pb", scatter_dimension=0, tiled=True)


def solution(mesh):
    return jax.shard_map(
        local,
        mesh=mesh,
        in_specs=(
            P("pb", "ka", None),
            P("pb", None, "ka"),
            P("pb", None, None),
            P("pb", None),
            P("pb", None),
            P(),
            P("pb", "ka"),
        ),
        out_specs=P("pb", "ka"),
        check_vma=False,
    )
```

```python
import functools

import jax
import jax.numpy as jnp
import numpy as np
from jax import lax
from jax.experimental import pallas as pl
from jax.experimental.pallas import tpu as pltpu
from jax.sharding import PartitionSpec as P

VB = 8
CB = 14
MESH = pl.DeviceIdType.MESH
NT = (((1,), (1,)), ((), ()))


def dot_nt(a, b):
    return lax.dot_general(a, b, NT, preferred_element_type=jnp.float32)


def halves(x):
    high = x.astype(jnp.bfloat16)
    return high, (x - high.astype(jnp.float32)).astype(jnp.bfloat16)


def ring_index(place, n):
    return jnp.where(place < n // 2, 2 * place, 2 * (n - 1 - place) + 1)


def kernel_blocks_kernel(
    n, parts, capacity,
    source_ref, v_ref, c_ref, w_ref, x_ref,
    k_ref, xout_ref,
    w_main, w_cross, v_all, v_high, v_low, stacked, b_high, b_low, k_part, k_near, k_go, k_got, x_all,
    local_sems, v_send, v_recv, ring_send, ring_recv, cross_send, cross_recv,
    near_send, near_recv, go_send, go_recv, x_send, x_recv, xk_send, xk_recv,
):
    pb, ka = lax.axis_index("pb"), lax.axis_index("ka")
    place = jnp.where(pb % 2 == 0, pb // 2, n - 1 - pb // 2)
    right = ring_index((place + 1) % n, n)
    left = ring_index((place + n - 1) % n, n)
    core = ka % 2
    partner = ka + 1 - 2 * core
    across = (ka + 2) % parts
    chip = ka - core
    other = (chip + 2) % parts
    rows = v_ref.shape[1]
    depth = w_main.shape[1]
    main = w_main.shape[2]
    half = depth // 2
    pairs = v_ref.shape[0]
    all_rows = parts * rows
    span = capacity * all_rows

    def at_block(index, count=1):
        return pl.ds(pl.multiple_of(index * depth, depth), count * depth)

    cross_rows = pl.ds(pl.multiple_of(core * half, half), half)
    loads = [
        pltpu.make_async_copy(w_ref.at[0, at_block(ka), at_block(ka)], w_main.at[place, :, pl.ds(0, depth)], local_sems.at[0]),
        pltpu.make_async_copy(
            w_ref.at[0, at_block(ka), at_block(other, 2)], w_main.at[place, :, pl.ds(depth, 2 * depth)], local_sems.at[1]
        ),
        pltpu.make_async_copy(
            w_ref.at[0, pl.ds(pl.multiple_of(chip * depth + core * half, half), half), at_block(chip + 1)],
            w_cross.at[place, cross_rows], local_sems.at[2],
        ),
        pltpu.make_async_copy(v_ref, v_all.at[ka], local_sems.at[3]),
    ]
    for load in loads:
        load.start()
    x_all[ka, pb] = x_ref[...]

    barrier = pltpu.get_barrier_semaphore()
    for d in range(1, n):
        pl.semaphore_signal(barrier, inc=1, device_id=((pb + d) % n, ka), device_id_type=MESH)
    for d in range(1, parts):
        pl.semaphore_signal(barrier, inc=1, device_id=(pb, (ka + d) % parts), device_id_type=MESH)
    pl.semaphore_wait(barrier, n + parts - 2)

    def remote(src, dst, send, recv, to):
        return pltpu.make_async_remote_copy(src_ref=src, dst_ref=dst, send_sem=send, recv_sem=recv, device_id=to, device_id_type=MESH)

    def ring(step):
        found = []
        for way, at, to in ((0, (place + n - step) % n, right), (1, (place + step) % n, left)):
            if step < n // 2 - 1:
                spans = (w_main.at[at], w_cross.at[at, cross_rows])
            else:
                quarter = half // 2
                spans = (
                    w_main.at[at, pl.ds(way * half, half)],
                    w_cross.at[at, pl.ds(pl.multiple_of(core * half + way * quarter, quarter), quarter)],
                )
            found.append([
                remote(part, part, ring_send.at[step, way, i], ring_recv.at[step, way, i], (to, ka)) for i, part in enumerate(spans)
            ])
        return found

    def cross_copy(at):
        part = w_cross.at[at, cross_rows]
        return remote(part, part, cross_send.at[at], cross_recv.at[at], (pb, partner))

    for load in loads:
        load.wait()
    v_across = remote(v_all.at[ka], v_all.at[ka], v_send.at[1], v_recv.at[1], (pb, across))
    v_partner = remote(v_all.at[ka], v_all.at[ka], v_send.at[0], v_recv.at[0], (pb, partner))
    v_pass = remote(v_all.at[across], v_all.at[across], v_send.at[2], v_recv.at[2], (pb, partner))
    copies = ring(0)
    for copy in copies[0] + copies[1]:
        copy.start()
    v_across.start()
    v_partner.start()
    cross_copy(place).start()
    x_copies = [
        remote(x_all.at[ka, pb], x_all.at[ka, pb], x_send.at[d - 1], x_recv.at[d - 1], ((pb + d) % n, ka)) for d in range(1, n)
    ]
    for copy in x_copies:
        copy.start()

    order = (ka, across, partner, (partner + 2) % parts)

    def split(kinds, p, carry):
        for i in kinds:
            pieces = ((at_block(ka), 0, depth), (at_block(other, 2), depth, 2 * depth), (at_block(partner), main, depth))
            for columns, at, size in pieces:
                high, low = halves(v_all[order[i], p, :, columns])
                v_high[p, pl.ds(i * rows, rows), pl.ds(at, size)] = high
                v_low[p, pl.ds(i * rows, rows), pl.ds(at, size)] = low
        return carry

    def place_of(k):
        return (place + n + ((k + 1) // 2) * (2 * (k % 2) - 1)) % n

    def near_copy(q):
        return remote(k_part.at[q, :, pl.ds(2 * rows, 2 * rows), :], k_near.at[q], near_send.at[q], near_recv.at[q], (pb, partner))

    def go_copy(q):
        return remote(k_go.at[q], k_got.at[q], go_send.at[q], go_recv.at[q], (pb, across))

    def pass_on(k):
        q = ring_index(place_of(k), n)
        near_copy(q).wait()
        for s in range(capacity):
            k_go[q, s] = k_part[q, s, pl.ds(rows, rows), :] + k_near[q, s, pl.ds(rows, rows), :]
        go_copy(q).start()

    def block(k):
        at = place_of(k)
        q = ring_index(at, n)
        for s in range(capacity):
            p = source_ref[q * capacity + s]
            stacked[pl.ds(s * all_rows, all_rows), :] = v_high[p]
            stacked[pl.ds(span + s * all_rows, all_rows), :] = v_low[p]
        high, low = halves(w_main[at])
        b_high[:, pl.ds(0, main)] = high
        b_low[:, pl.ds(0, main)] = low
        cross_copy(at).wait()
        between = w_cross[at]
        high, low = halves(jnp.where(core == 0, between, between.T))
        b_high[:, pl.ds(main, depth)] = high
        b_low[:, pl.ds(main, depth)] = low
        both = dot_nt(stacked[...], b_high[...])
        screened = both[:span] + (both[span:] + dot_nt(stacked[pl.ds(0, span), :], b_low[...]))
        s_high, s_low = halves(screened)
        for s in range(capacity):
            part = slice(s * all_rows, (s + 1) * all_rows)
            conduct = c_ref[source_ref[q * capacity + s]]
            k_part[q, s] = dot_nt(s_high[part], conduct) + dot_nt(s_low[part], conduct)
        near_copy(q).start()

    def blocks(first, last):
        def one(k, carry):
            block(k)
            pass_on(k - 1)
            return carry

        lax.fori_loop(first, last, one, 0)

    v_partner.wait()
    lax.fori_loop(0, pairs, functools.partial(split, (0, 2)), 0)
    for step in range(1, n // 2):
        later = ring(step)
        for way in range(2):
            for landed, follow in zip(copies[way], later[way]):
                landed.wait_recv()
                follow.start()
            cross_copy(place_of(2 * step - way)).start()
        for copy in copies[0] + copies[1]:
            copy.wait_send()
        copies = later
        if step == 1:
            for copy in x_copies:
                copy.wait()
            xk_copies = [
                remote(x_all.at[ka], x_all.at[ka], xk_send.at[d - 1], xk_recv.at[d - 1], (pb, (ka + d) % parts))
                for d in range(1, parts)
            ]
            for copy in xk_copies:
                copy.start()
        if step == n // 2 - 2:
            v_across.wait()
            v_pass.start()
            v_pass.wait()
            lax.fori_loop(0, pairs, functools.partial(split, (1, 3)), 0)
            block(0)
            blocks(1, n - 5)
            for copy in xk_copies:
                copy.wait()
            xout_ref[...] = x_all[...]
        if step == n // 2 - 1:
            blocks(n - 5, n - 1)
    for copy in copies[0] + copies[1]:
        copy.wait()
    cross_copy(place_of(n - 1)).start()
    blocks(n - 1, n)
    pass_on(n - 1)

    def total(q, carry):
        go_copy(q).wait()
        for s in range(capacity):
            k_ref[q, s] = (k_part[q, s, pl.ds(0, rows), :] + k_near[q, s, pl.ds(0, rows), :]) + k_got[q, s]
        return carry

    lax.fori_loop(0, n, total, 0)


def response_kernel(
    n, parts,
    position_ref, kpairs_ref, slot_ref, k_ref, x_ref, mask_ref, spread_ref, near_ref, pick_ref,
    out_ref,
    wide_rows, mixed, by_far, x_high, x_low, given, landed, joined, landed_pb,
    ka_send, ka_recv, pb_send, pb_recv,
):
    pb, ka = lax.axis_index("pb"), lax.axis_index("ka")
    trials, wide = x_ref.shape[2:]
    full = spread_ref.shape[2]
    tall = mask_ref.shape[0]
    local_v = k_ref.shape[1] // VB
    band = local_v * tall
    pairs = position_ref.shape[0]
    barrier = pltpu.get_barrier_semaphore()
    for d in range(1, n):
        pl.semaphore_signal(barrier, inc=1, device_id=((pb + d) % n, ka), device_id_type=MESH)
    for d in range(1, parts):
        pl.semaphore_signal(barrier, inc=1, device_id=(pb, (ka + d) % parts), device_id_type=MESH)

    def dot(a, b):
        return jnp.dot(a, b, preferred_element_type=jnp.float32)

    x_high[...] = jnp.zeros_like(x_high)
    x_low[...] = jnp.zeros_like(x_low)
    for m in range(n):
        for j in range(parts):
            high, low = halves(x_ref[j, m])
            x_high[pl.ds(j * trials, trials), pl.ds(m * full, wide)] = high
            x_low[pl.ds(j * trials, trials), pl.ds(m * full, wide)] = low

    def fill(p, carry):
        values = k_ref[position_ref[p]]
        for w in range(VB):
            for v in range(local_v):
                row = values[v * VB + w:v * VB + w + 1]
                high, low = halves(jnp.broadcast_to(row, mask_ref.shape) * mask_ref[...])
                wide_rows[w, p, pl.ds(v * tall, tall), :] = high
                wide_rows[w, pairs + p, pl.ds(v * tall, tall), :] = low
        return carry

    lax.fori_loop(0, pairs, fill, 0)
    lanes = wide_rows.shape[-1]
    for w in range(VB):
        part = dot(wide_rows[w].reshape(2 * pairs * band, lanes), spread_ref[w])
        if w == 0:
            mixed[...] = part
        else:
            mixed[...] += part

    def cut(p, carry):
        at = pl.multiple_of(p * band, band)
        value = mixed[pl.ds(at, band), :] + mixed[pl.ds(pl.multiple_of((pairs + p) * band, band), band), :]
        far = slot_ref[kpairs_ref[p, 1]]
        for m in range(n):
            high, low = halves(value * (far == m).astype(jnp.float32))
            by_far[0, pl.ds(at, band), pl.ds(m * full, full)] = high
            by_far[1, pl.ds(at, band), pl.ds(m * full, full)] = low
        return carry

    lax.fori_loop(0, pairs, cut, 0)
    g_high, g_low = halves(dot(near_ref[...], by_far[0]) + dot(near_ref[...], by_far[1]))
    pick = pick_ref[...]
    p_high = dot_nt(x_high[...], pick).astype(jnp.bfloat16)
    p_low = dot_nt(x_low[...], pick).astype(jnp.bfloat16)
    direct = dot_nt(x_high[...], g_high) + (dot_nt(x_high[...], g_low) + dot_nt(x_low[...], g_high))
    d_high, d_low = halves(direct)
    value = dot(p_high, g_high) + (dot(p_high, g_low) + dot(p_low, g_high))
    value = value + (dot(d_high, pick) + dot(d_low, pick))
    for m in range(n):
        for j in range(parts):
            given[m, j] = value[j * trials:(j + 1) * trials, m * full:(m + 1) * full]
    pl.semaphore_wait(barrier, n + parts - 2)

    def remote(src, dst, send, recv, to):
        return pltpu.make_async_remote_copy(src_ref=src, dst_ref=dst, send_sem=send, recv_sem=recv, device_id=to, device_id_type=MESH)

    def ka_copy(m, d):
        to = (ka + d) % parts
        return remote(given.at[m, to], landed.at[d - 1, m], ka_send.at[m, d - 1], ka_recv.at[m, d - 1], (pb, to))

    def pb_copy(d):
        to = (pb + d) % n
        return remote(joined.at[to], landed_pb.at[d - 1], pb_send.at[d - 1], pb_recv.at[d - 1], (to, ka))

    def send(m, carry):
        for d in range(1, parts):
            ka_copy(m, d).start()
        return carry

    lax.fori_loop(0, n, send, 0)

    def join(m, carry):
        value = given[m, ka]
        for d in range(1, parts):
            ka_copy(m, d).wait()
            value = value + landed[d - 1, m]
        joined[m] = value
        return carry

    lax.fori_loop(0, n, join, 0)
    for d in range(1, n):
        pb_copy(d).start()
    value = joined[pb]
    for d in range(1, n):
        pb_copy(d).wait()
        value = value + landed_pb[d - 1]
    out_ref[...] = value[:, :wide]


def ringed(valence, conduction, screened, momentum, kpairs, kpoint_slot, trial_blocks):
    pair_dev, rows, waves = valence.shape
    n, parts = lax.axis_size("pb"), lax.axis_size("ka")
    capacity, slot_count, position, source = slots(momentum, pair_dev, n)
    trials = trial_blocks.shape[1] // (VB * CB)
    wide = VB * CB
    depth = conduction.shape[2]
    columns = conduction.shape[1]
    vmem = pl.BlockSpec(memory_space=pltpu.VMEM)
    any_space = pl.BlockSpec(memory_space=pl.ANY)
    dma = pltpu.SemaphoreType.DMA
    kernel, x_all = pl.pallas_call(
        functools.partial(kernel_blocks_kernel, n, parts, capacity),
        out_shape=(
            jax.ShapeDtypeStruct((n, capacity, rows, columns), jnp.float32),
            jax.ShapeDtypeStruct((parts, n, trials, wide), jnp.float32),
        ),
        in_specs=[pl.BlockSpec(memory_space=pltpu.SMEM), any_space, vmem, any_space, vmem],
        out_specs=(vmem, vmem),
        scratch_shapes=[
            pltpu.VMEM((n, depth, waves - depth), jnp.float32),
            pltpu.VMEM((n, depth, depth), jnp.float32),
            pltpu.VMEM((parts, pair_dev, rows, waves), jnp.float32),
            pltpu.VMEM((pair_dev, parts * rows, waves), jnp.bfloat16),
            pltpu.VMEM((pair_dev, parts * rows, waves), jnp.bfloat16),
            pltpu.VMEM((2 * capacity * parts * rows, waves), jnp.bfloat16),
            pltpu.VMEM((depth, waves), jnp.bfloat16),
            pltpu.VMEM((depth, waves), jnp.bfloat16),
            pltpu.VMEM((n, capacity, parts * rows, columns), jnp.float32),
            pltpu.VMEM((n, capacity, 2 * rows, columns), jnp.float32),
            pltpu.VMEM((n, capacity, rows, columns), jnp.float32),
            pltpu.VMEM((n, capacity, rows, columns), jnp.float32),
            pltpu.VMEM((parts, n, trials, wide), jnp.float32),
            dma((4,)), dma((3,)), dma((3,)), dma((n // 2, 2, 2)), dma((n // 2, 2, 2)), dma((n,)), dma((n,)),
            dma((n,)), dma((n,)), dma((n,)), dma((n,)), dma((n - 1,)), dma((n - 1,)), dma((parts - 1,)), dma((parts - 1,)),
        ],
        compiler_params=pltpu.CompilerParams(collective_id=0, has_side_effects=True, vmem_limit_bytes=56 * 1024 * 1024),
    )(source, valence, conduction, screened, trial_blocks.reshape(trials, wide))
    ka = lax.axis_index("ka")
    local_v = rows // VB
    tall = -(-CB // 16) * 16
    band = local_v * tall
    every = parts * trials
    full = -(-wide // 128) * 128
    c_of, d_of = np.arange(columns) // CB, np.arange(columns) % CB
    lane = np.arange(full)
    w_to, d_to = lane // CB, lane % CB
    mask = (np.arange(tall)[:, None] == c_of[None, :]).astype(np.float32)
    at_w = (w_to[None, None, :] == np.arange(VB)[:, None, None]) & (lane < wide)[None, None, :]
    spread = ((d_of[:, None] == d_to[None, :])[None] & at_w).astype(jnp.bfloat16)
    band_row = np.arange(n * band)
    k_row, v_row, c_row = band_row // band, band_row % band // tall, band_row % tall
    all_lane = np.arange(n * full)
    same_c = (k_row[:, None] == all_lane[None, :] // full) & (c_row[:, None] == all_lane[None, :] % full % CB)
    lane_v = np.where(all_lane % full < wide, all_lane % full // CB, -1).astype(np.int32)
    pick = jnp.where(jnp.asarray(same_c) & ((ka * local_v + jnp.asarray(v_row, jnp.int32))[:, None] == jnp.asarray(lane_v)[None, :]), 1.0, 0.0)
    pair_row = np.arange(pair_dev * band)
    same_row = band_row[:, None] % band == pair_row[None, :] % band
    slot_near = jnp.take(kpoint_slot, kpairs[:, 0])
    near_lane = jnp.repeat(slot_near, band)
    near = jnp.where(jnp.asarray(same_row) & (near_lane[None, :] == jnp.asarray(k_row, jnp.int32)[:, None]), 1.0, 0.0)
    smem = pl.BlockSpec(memory_space=pltpu.SMEM)
    result = pl.pallas_call(
        functools.partial(response_kernel, n, parts),
        out_shape=jax.ShapeDtypeStruct((trials, wide), jnp.float32),
        in_specs=[smem] * 3 + [vmem] * 6,
        out_specs=vmem,
        scratch_shapes=[
            pltpu.VMEM((VB, 2 * pair_dev, band, columns), jnp.bfloat16),
            pltpu.VMEM((2 * pair_dev * band, full), jnp.float32),
            pltpu.VMEM((2, pair_dev * band, n * full), jnp.bfloat16),
            pltpu.VMEM((every, n * full), jnp.bfloat16),
            pltpu.VMEM((every, n * full), jnp.bfloat16),
            pltpu.VMEM((n, parts, trials, full), jnp.float32),
            pltpu.VMEM((parts - 1, n, trials, full), jnp.float32),
            pltpu.VMEM((n, trials, full), jnp.float32),
            pltpu.VMEM((n - 1, trials, full), jnp.float32),
            dma((n, parts - 1)), dma((n, parts - 1)), dma((n - 1,)), dma((n - 1,)),
        ],
        compiler_params=pltpu.CompilerParams(collective_id=1, has_side_effects=True, vmem_limit_bytes=48 * 1024 * 1024),
    )(
        position, kpairs, kpoint_slot, kernel.reshape(slot_count, rows, columns), x_all,
        jnp.asarray(mask), jnp.asarray(spread), near.astype(jnp.bfloat16), pick.astype(jnp.bfloat16),
    )
    return result.reshape(1, trials * wide)


def slots(momentum, pair_dev, owners):
    capacity = max(2, 2 * pair_dev // owners)
    slot_count = owners * capacity
    target = momentum[:, 0]
    indices = jnp.arange(pair_dev, dtype=jnp.int32)
    earlier = (target[:, None] == target[None, :]) & (indices[None, :] < indices[:, None])
    position = target * capacity + jnp.sum(earlier.astype(jnp.int32), axis=1)
    matches = position[None, :] == jnp.arange(slot_count, dtype=jnp.int32)[:, None]
    source = jnp.sum(jnp.where(matches, indices[None, :], 0), axis=1)
    return capacity, slot_count, position, source


def local(valence, conduction, screened, momentum, kpairs, kpoint_slot, trial_blocks):
    n, parts = lax.axis_size("pb"), lax.axis_size("ka")
    if n >= 8 and n % 2 == 0 and parts == 4 and n * conduction.shape[2] * valence.shape[2] * 4 <= 16 * 1024 * 1024:
        return ringed(valence, conduction, screened, momentum, kpairs, kpoint_slot, trial_blocks)
    return routed(valence, conduction, screened, momentum, kpairs, kpoint_slot, trial_blocks)


def routed(valence, conduction, screened, momentum, kpairs, kpoint_slot, trial_blocks):
    highest = lax.Precision.HIGHEST
    pair_dev = valence.shape[0]
    owners = lax.axis_size("pb")
    capacity = max(2, 2 * pair_dev // owners)
    slot_count = owners * capacity
    target = momentum[:, 0]
    indices = jnp.arange(pair_dev, dtype=jnp.int32)
    earlier = (target[:, None] == target[None, :]) & (indices[None, :] < indices[:, None])
    position = target * capacity + jnp.sum(earlier.astype(jnp.int32), axis=1)
    matches = position[None, :] == jnp.arange(slot_count, dtype=jnp.int32)[:, None]
    source = jnp.sum(jnp.where(matches, indices[None, :], 0), axis=1)
    filled = jnp.any(matches, axis=1)
    outgoing = jnp.where(filled[:, None, None], jnp.take(valence, source, axis=0), 0.0)
    outgoing = outgoing.reshape(owners, capacity, valence.shape[1], valence.shape[2])
    matrix = screened[0]
    product = jnp.einsum(
        "scrg,gh->scrh",
        lax.all_to_all(outgoing, "pb", split_axis=0, concat_axis=0, tiled=True),
        matrix,
        precision=highest,
        preferred_element_type=jnp.float32,
    )
    returned = lax.all_to_all(product, "pb", split_axis=0, concat_axis=0, tiled=True)
    by_slot = returned.reshape(slot_count, returned.shape[2], returned.shape[3])
    rows_back = jnp.take(by_slot, position, axis=0)
    columns = lax.all_to_all(rows_back, "ka", split_axis=2, concat_axis=1, tiled=True)
    conduct_wide = conduction.astype(jnp.float32)
    partial_kernel = jnp.einsum(
        "prg,pbg->prb", columns, conduct_wide, precision=highest, preferred_element_type=jnp.float32
    )
    kernel = lax.psum(partial_kernel, "ka")
    gathered = lax.all_gather(trial_blocks, "pb", axis=0, tiled=True)
    kpoint_count = gathered.shape[0]
    local_trials = gathered.shape[1] // (VB * CB)
    blocks = gathered.reshape(kpoint_count, local_trials, VB, CB)
    slot_near = jnp.take(kpoint_slot, kpairs[:, 0])
    slot_far = jnp.take(kpoint_slot, kpairs[:, 1])
    near_trials = jnp.take(blocks, slot_near, axis=0)
    far_trials = jnp.take(blocks, slot_far, axis=0)
    kernel_blocks = kernel.reshape(pair_dev, VB, VB, CB, CB)
    direct = jnp.einsum("pvwcd,pnwd->pnvc", kernel_blocks, far_trials, precision=highest)
    mirror = jnp.einsum("pvwcd,pnvc->pnwd", kernel_blocks, near_trials, precision=highest)
    kpoint_rows = jnp.arange(kpoint_count, dtype=jnp.int32)[:, None]
    onehot_near = (slot_near[None, :] == kpoint_rows).astype(jnp.float32)
    onehot_far = (slot_far[None, :] == kpoint_rows).astype(jnp.float32)
    summed = jnp.dot(
        onehot_near,
        direct.reshape(pair_dev, -1),
        precision=highest,
        preferred_element_type=jnp.float32,
    )
    summed = summed + jnp.dot(
        onehot_far,
        mirror.reshape(pair_dev, -1),
        precision=highest,
        preferred_element_type=jnp.float32,
    )
    return lax.psum_scatter(summed, "pb", scatter_dimension=0, tiled=True)


def solution(mesh):
    return jax.shard_map(
        local,
        mesh=mesh,
        in_specs=(
            P("pb", "ka", None),
            P("pb", None, "ka"),
            P("pb", None, None),
            P("pb", None),
            P("pb", None),
            P(),
            P("pb", "ka"),
        ),
        out_specs=P("pb", "ka"),
        check_vma=False,
    )
```
